128 devices in a mesh: dp: 32 (over x_lo, y, z), section: 4 (over x_hi, core).
Axes of the slice: x: 4 (x_hi: 2, x_lo: 2; x = x_hi * 2 + x_lo), y: 4, z: 4, core: 2. Of those that a mesh axis runs over, the one named last changes fastest.
Arguments:
- hidden_in: bfloat16 [64, 64, 4096], P('dp'), may hold values from -6 to 6
- targets: bfloat16 [64, 64, 4096], P('dp'), may hold values from -6 to 6
- down_factors: bfloat16 [4, 2, 128, 4096], P('section', None, None, 'dp'), may hold values from -0.09375 to 0.09375
- up_factors: bfloat16 [4, 4, 128, 4096], P('section', None, None, 'dp'), may hold values from -18 to 18
- down_dir: bfloat16 [4, 2, 128, 4096], P('section', None, None, 'dp'), may hold values from -0.09375 to 0.09375
- up_dir: bfloat16 [4, 4, 128, 4096], P('section', None, None, 'dp'), may hold values from -0.5 to 0.5
Outputs:
- hv_down: float32 [4, 2, 128, 4096], P('section', None, None, 'dp')
- hv_up: float32 [4, 4, 128, 4096], P('section', None, None, 'dp')
The draws below stay inside these ranges and needn't reach their ends.
All inputs are finite; a program needn't handle non-finite values.
Results may differ from the reference program's by a relative error of at most 0.025.
Values may be sent and summed in bfloat16 or wider, within the bound.
A program may use at most 192 MiB of HBM per device.

```python
import math
import jax
import jax.numpy as jnp
from jax import lax

D = 4096
HEAD_DIM = 128
RANK = 128
TOK = 64
MICRO = 2
SECTIONS = 4
SEQS = 64
N_DP = 32


def draw_up_factors(key, part):
    base = jax.random.truncated_normal(key, -6.0, 6.0, (SECTIONS, 4, RANK, D), jnp.float32) * RANK ** (-0.5)
    return base.astype(jnp.bfloat16)


def shard_levels(own_key, extent, pieces, low, high):
    gain, own = 1.0, jax.random.fold_in(own_key, 6)
    for axis_at, shards_of in pieces:
        heights = jnp.exp(jax.random.uniform(jax.random.fold_in(own, axis_at), (shards_of,), jnp.float32, low / len(pieces), high / len(pieces)))
        gain = gain * jnp.repeat(heights, extent[axis_at] // shards_of).reshape([-1 if axis == axis_at else 1 for axis in range(len(extent))])
    return gain


def gaussian(rng, shape, scale, most, split=(), kind=jnp.bfloat16):
    entries = jax.random.normal(rng, shape, jnp.float32) * scale
    if len(split) > 0:
        entries = shard_levels(rng, shape, split, -0.22, 0.18) * entries
    return jnp.clip(entries, min=-most, max=most).astype(kind)


def setup_inputs(seed: int = 0) -> dict:
    key_list = jax.random.split(jax.random.key(seed), 7)
    return {
        "hidden_in": gaussian(key_list[0], (SEQS, TOK, D), 1.0, 6.0, ((0, 32),)),
        "targets": gaussian(key_list[1], (SEQS, TOK, D), 1.0, 6.0, ((0, 32),)),
        "down_factors": gaussian(key_list[2], (SECTIONS, 2, RANK, D), D ** -0.5, 0.09375, ((0, 4), (3, 32))),
        "up_factors": draw_up_factors(jax.random.fold_in(key_list[6], 71), 0),
        "down_dir": gaussian(key_list[4], (SECTIONS, 2, RANK, D), D ** -0.5, 0.09375, ((0, 4), (3, 32))),
        "up_dir": gaussian(key_list[5], (SECTIONS, 4, RANK, D), RANK ** -0.5, 0.5, ((0, 4), (3, 32))),
    }


EPS = 1e-05

def layer_step(hidden, down_set, up_set):
    tokens = hidden.shape[0]
    head_count = hidden.shape[1] // HEAD_DIM
    widened = hidden.astype(jnp.float32)
    normed = (widened * lax.rsqrt(lax.optimization_barrier(jnp.mean(widened * widened, axis=-1, keepdims=True)) + EPS)).astype(jnp.bfloat16)
    contract = (((1,), (1,)), ((), ()))
    latent = lax.dot_general(normed, down_set[0], contract, preferred_element_type=jnp.float32).astype(jnp.bfloat16)
    queries = jnp.dot(latent, up_set[0], preferred_element_type=jnp.float32).astype(jnp.bfloat16)
    key_rows = jnp.dot(latent, up_set[1], preferred_element_type=jnp.float32).astype(jnp.bfloat16)
    values = jnp.dot(latent, up_set[2], preferred_element_type=jnp.float32).astype(jnp.bfloat16)
    query_heads = queries.reshape(tokens, head_count, HEAD_DIM).astype(jnp.float32)
    key_heads = key_rows.reshape(tokens, head_count, HEAD_DIM).astype(jnp.float32)
    value_heads = values.reshape(tokens, head_count, HEAD_DIM).astype(jnp.float32)
    scores = jnp.einsum('qhd,khd->hqk', query_heads, key_heads) / math.sqrt(HEAD_DIM)
    causal = jnp.arange(tokens)[:, None] >= jnp.arange(tokens)[None, :]
    scores = jnp.where(causal[None], scores, -1e+30)
    row_max = lax.optimization_barrier(jnp.max(scores, axis=-1, keepdims=True))
    exponent = jnp.exp(scores - row_max)
    attn_weights = (exponent / lax.optimization_barrier(jnp.sum(exponent, axis=-1, keepdims=True))).astype(jnp.bfloat16)
    mixed_heads = jnp.einsum('hqk,khd->qhd', attn_weights.astype(jnp.float32), value_heads)
    mixed_heads = mixed_heads.astype(jnp.bfloat16).reshape(tokens, head_count * HEAD_DIM)
    merged = lax.dot_general(mixed_heads, down_set[1], contract, preferred_element_type=jnp.float32).astype(jnp.bfloat16)
    branch = jnp.dot(merged, up_set[3], preferred_element_type=jnp.float32)
    return (widened + branch).astype(jnp.bfloat16)

def sequence_loss(final, target_seq, count_total):
    diff_rows = final.astype(jnp.float32) - target_seq.astype(jnp.float32)
    return 0.5 * jnp.sum(diff_rows * diff_rows) / count_total

def reference(hidden_in, targets, down_factors, up_factors, down_dir, up_dir):
    count_total = N_DP * MICRO * TOK

    def total_loss(down_wide, up_wide):

        def one_sequence(carry, pair):
            current = pair[0]
            for section_idx in range(SECTIONS):
                current = layer_step(current, down_wide[section_idx].astype(jnp.bfloat16), up_wide[section_idx].astype(jnp.bfloat16))
            return (carry + sequence_loss(current, pair[1], count_total), None)
        summed, _ = lax.scan(one_sequence, jnp.zeros((), jnp.float32), (hidden_in, targets))
        return summed
    gradient = jax.grad(total_loss, argnums=(0, 1))
    _, curvature = jax.jvp(gradient, (down_factors.astype(jnp.float32), up_factors.astype(jnp.float32)), (down_dir.astype(jnp.float32), up_dir.astype(jnp.float32)))
    return (curvature[0], curvature[1])
```

```python
import functools
import math

import jax
import jax.numpy as jnp
from jax import lax
from jax.experimental import pallas as pl
from jax.experimental.pallas import tpu as pltpu
from jax.sharding import PartitionSpec as P

EPS = 1e-05
MESH = pl.DeviceIdType.MESH
F32 = jnp.float32
BF16 = jnp.bfloat16


def dot_nt(a, b):
    return lax.dot_general(a, b, (((1,), (1,)), ((), ())), preferred_element_type=F32)


def dot_tn(a, b):
    return lax.dot_general(a, b, (((0,), (0,)), ((), ())), preferred_element_type=F32)


def dot_nn(a, b):
    return lax.dot_general(a, b, (((1,), (0,)), ((), ())), preferred_element_type=F32)


def lower(a, at):
    return jnp.concatenate(
        [jnp.concatenate([a, jnp.zeros_like(a)], 1), jnp.concatenate([at, a], 1)], 0
    )


def cross(full):
    n, m = full.shape[0] // 2, full.shape[1] // 2
    return full[:n, :m], full[:n, m:] + full[n:, :m]


def head_forward(q2, k2, v2, mask, scale):
    s, st = cross(dot_nt(q2, k2))
    s = jnp.where(mask, s * scale, -1e30)
    st = st * scale
    e = jnp.exp(s - jnp.max(s, axis=-1, keepdims=True))
    w = e / jnp.sum(e, axis=-1, keepdims=True)
    wt = w * (st - jnp.sum(w * st, axis=-1, keepdims=True))
    w, wt = w.astype(BF16), wt.astype(BF16)
    return w, wt, dot_nn(lower(w, wt), v2)


def head_backward(q2, k2, v2, w, wt, dm2, scale):
    n = w.shape[0]
    da, dat = cross(dot_nt(dm2, v2))
    dvs = dot_tn(lower(w, wt), jnp.concatenate([dm2[n:], dm2[:n]], 0))
    wf, wtf = w.astype(F32), wt.astype(F32)
    da = da - jnp.sum(wf * da, axis=-1, keepdims=True)
    wda = wf * da
    dst = wtf * da + wf * dat
    dst = dst - wf * jnp.sum(dst, axis=-1, keepdims=True)
    ds = (wda * scale).astype(BF16)
    dst = (dst * scale).astype(BF16)
    low = lower(ds, dst)
    dq2 = dot_nn(low, k2)
    dks = dot_tn(low, jnp.concatenate([q2[n:], q2[:n]], 0))
    return (
        dq2,
        jnp.concatenate([dks[n:], dks[:n]], 0),
        jnp.concatenate([dvs[n:], dvs[:n]], 0),
    )


def kernel(
    dims,
    hy_ref, df_ref, uf_ref, dd_ref, ud_ref,
    down_ref, up_ref,
    W, HY, H2, QKV, AW, MIX, AS, RR, MS, LS, G2, DX, DMIX, GR,
    snd, rcv, RB0, RH, RF, P1, RH2, RF2,
    own_sem, s1, r1, s2, r2, s3, r3, hs, hr, ars, arr, sa, ra, sb, rb, sc, rc,
):
    R, HD, TOK, D, count = dims
    T = 2 * TOK
    C = 8 * HD
    CH = 2 * HD
    dp = lax.axis_index("dp")
    sec = lax.axis_index("section")
    x = 2 * (sec // 2) + dp // 16
    y = (dp // 4) % 4
    z = dp % 4
    c = sec % 2

    def dev(x, y, z, c):
        return ((x % 2) * 16 + y * 4 + z, (x // 2) * 2 + c)

    def to_xy(p1, p2):
        return p1 * (1 - c) + p2 * c, p2 * (1 - c) + p1 * c

    p1 = x * (1 - c) + y * c
    p2 = y * (1 - c) + x * c

    def devp(q1, q2):
        xx, yy = to_xy(q1 % 4, q2 % 4)
        return dev(xx, yy, z, c)

    def piece(ref, q1, q2, f0, f1):
        xx, yy = to_xy(q1 % 4, q2 % 4)
        col = pl.multiple_of(((xx % 2) * 4 + yy) * HD, HD)
        return ref.at[2 * (xx // 2) + c, f0:f1, :, pl.ds(col, HD)]

    sibling = dev(x, y, z, 1 - c)

    def send(src, dst, ssem, rsem, to):
        copy = pltpu.make_async_remote_copy(
            src_ref=src, dst_ref=dst, send_sem=ssem, recv_sem=rsem,
            device_id=to, device_id_type=MESH,
        )
        copy.start()
        return copy

    mine = [
        pltpu.make_async_copy(df_ref.at[0], piece(W, p1, p2, 0, 2).at[:, 0:R], own_sem.at[0]),
        pltpu.make_async_copy(dd_ref.at[0], piece(W, p1, p2, 0, 2).at[:, R : 2 * R], own_sem.at[1]),
        pltpu.make_async_copy(uf_ref.at[0], piece(W, p1, p2, 2, 6).at[:, 0:R], own_sem.at[2]),
        pltpu.make_async_copy(ud_ref.at[0], piece(W, p1, p2, 2, 6).at[:, R : 2 * R], own_sem.at[3]),
    ]
    for copy in mine:
        copy.start()

    barrier = pltpu.get_barrier_semaphore()
    peers = [
        devp(p1 + 1, p2), devp(p1 - 1, p2), devp(p1, p2 + 1), devp(p1, p2 - 1), sibling,
        dev(x, y, (z + 1) % 4, c), dev(x, y, (z + 2) % 4, c), dev(x, y, (z + 3) % 4, c),
    ]
    for peer in peers:
        pl.semaphore_signal(barrier, inc=1, device_id=peer, device_id_type=MESH)
    pl.semaphore_wait(barrier, len(peers))

    half = z // 2

    @pl.when(z % 2 == c)
    def _():
        keep = pltpu.make_async_copy(hy_ref.at[z], HY.at[:, half], hr.at[half])
        keep.start()
        out = []
        for d in (1, 2, 3):
            to = (z + d) % 4
            out.append(
                send(hy_ref.at[to], HY.at[:, half], hs.at[d - 1], hr.at[half], dev(x, y, to, c))
            )
        for copy in out:
            copy.wait_send()

    for copy in mine:
        copy.wait()

    sent = []

    def ring_send(q1, q2, ssem, rsem, axis):
        for i, d in enumerate((1, -1)):
            to = devp(p1 + d, p2) if axis == 1 else devp(p1, p2 + d)
            sent.append(
                send(piece(W, q1, q2, 0, 6), piece(W, q1, q2, 0, 6), ssem(i), rsem(i), to)
            )

    def forward(i, q1, q2, ssem, rsem, axis):
        d = (1, -1)[i]
        to = devp(p1 + d, p2) if axis == 1 else devp(p1, p2 + d)
        f0, f1 = ((0, 3), (3, 6))[i]
        sent.append(
            send(piece(W, q1, q2, f0, f1), piece(W, q1, q2, f0, f1), ssem(2 + i), rsem(2 + i), to)
        )

    def expect(q1, q2, f0, f1, rsem):
        ref = piece(W, q1, q2, f0, f1)
        pltpu.make_async_copy(ref, ref, rsem).wait()

    def share(i, q1, q2):
        sent.append(
            send(piece(W, q1, q2, 0, 6), piece(W, q1, q2, 0, 6), s3.at[i], r3.at[i], sibling)
        )

    offs = (0, -1, 1, 2)

    def start_second(k):
        q1 = p1 + offs[k]
        ring_send(q1, p2, lambda i: s2.at[4 * k + i], lambda i: r2.at[4 * k + i], 2)
        share(4 * k, q1, p2)

    def relay_second(k):
        q1 = p1 + offs[k]
        for i, d in enumerate((-1, 1)):
            expect(q1, p2 + d, 0, 6, r2.at[4 * k + i])
            forward(i, q1, p2 + d, lambda j: s2.at[4 * k + j], lambda j: r2.at[4 * k + j], 2)
            share(4 * k + 1 + i, q1, p2 + d)

    def end_second(k):
        q1 = p1 + offs[k]
        expect(q1, p2 + 2, 0, 3, r2.at[4 * k + 2])
        expect(q1, p2 + 2, 3, 6, r2.at[4 * k + 3])
        share(4 * k + 3, q1, p2 + 2)

    ring_send(p1, p2, lambda i: s1.at[i], lambda i: r1.at[i], 1)
    start_second(0)
    for i, d in enumerate((-1, 1)):
        expect(p1 + d, p2, 0, 6, r1.at[i])
        forward(i, p1 + d, p2, lambda j: s1.at[j], lambda j: r1.at[j], 1)
        start_second(1 + i)
    relay_second(0)
    expect(p1 + 2, p2, 0, 3, r1.at[2])
    expect(p1 + 2, p2, 3, 6, r1.at[3])
    start_second(3)
    relay_second(1)
    relay_second(2)
    end_second(0)
    relay_second(3)
    end_second(1)
    end_second(2)
    end_second(3)

    for i in range(2):
        ref = HY.at[:, i]
        pltpu.make_async_copy(ref, ref, hr.at[i]).wait()
    for i in range(16):
        ref = piece(W, p1, p2, 0, 6)
        pltpu.make_async_copy(ref, ref, r3.at[i]).wait()

    row = lax.broadcasted_iota(jnp.int32, (T, T), 0)
    col = lax.broadcasted_iota(jnp.int32, (T, T), 1)
    eye = row == col
    mask = (row >= col) & ((row < TOK) == (col < TOK))
    scale = 1.0 / math.sqrt(HD)

    def to_row(column):
        return jnp.sum(jnp.where(eye, column, 0.0), axis=0, keepdims=True)

    def to_column(line):
        return jnp.sum(jnp.where(eye, line, 0.0), axis=1, keepdims=True)

    def reduce_start(par, rows):
        copies = []
        for d in (1, 2, 3):
            copies.append(
                send(
                    snd.at[par, 0:rows], rcv.at[par, d - 1, 0:rows],
                    ars.at[par, d - 1], arr.at[par, d - 1], dev(x, y, (z + d) % 4, c),
                )
            )
        return copies

    def reduce_end(par, rows, copies):
        for copy in copies:
            copy.wait()
        total = snd[par, 0:rows].astype(F32)
        for d in range(3):
            total = total + rcv[par, d, 0:rows].astype(F32)
        return total

    def put(par, value, tangent):
        snd[par, 0:T, 0:R] = value.astype(BF16)
        snd[par, 0:T, R : 2 * R] = tangent.astype(BF16)

    chunks = [slice(j, j + CH) for j in range(0, C, CH)]

    for i in range(2):
        H2[0, i * TOK : (i + 1) * TOK] = HY[0, i]
    H2[0, T : 2 * T] = jnp.zeros((T, C), BF16)

    def forward_layer(s, carry):
        full = jnp.zeros((2 * T, 2 * R), F32)
        ss = jnp.zeros((T, 1), F32)
        st = jnp.zeros((T, 1), F32)
        for ch in chunks:
            h2 = H2[s, :, ch]
            full = full + dot_nt(h2, W[s, 0, :, ch])
            hf = h2[:T].astype(F32)
            ss = ss + jnp.sum(hf * hf, axis=1, keepdims=True)
            st = st + jnp.sum(hf * h2[T:].astype(F32), axis=1, keepdims=True)
        put(0, *cross(full))
        line = jnp.concatenate([to_row(ss), to_row(st)], 1)
        high = line.astype(BF16).astype(F32)
        place = lax.broadcasted_iota(jnp.int32, (16, 2 * T), 0)
        pair = jnp.where(place == 0, high, jnp.where(place == 1, line - high, 0.0))
        snd[0, T : T + 16, :] = pair.astype(BF16)
        total = reduce_end(0, T + 16, reduce_start(0, T + 16))
        line = jnp.sum(total[T:], axis=0, keepdims=True)
        ss, st = to_column(line[:, :T]), to_column(line[:, T:])
        r = lax.rsqrt(ss / D + EPS)
        rt = -(r * r * r) * st / D
        a, at = total[:T, :R], total[:T, R:]
        AS[s] = total[:T]
        RR[s, 0] = jnp.broadcast_to(r, (T, R))
        RR[s, 1] = jnp.broadcast_to(rt, (T, R))
        lat = (r * a).astype(BF16)
        latt = (r * at + rt * a).astype(BF16)
        LS[s, 0:T] = latt
        LS[s, T : 2 * T] = lat
        low = lower(lat, latt)
        for f in range(3):
            for ch in chunks:
                QKV[s, f, :, ch] = dot_nn(low, W[s, 2 + f, :, ch]).astype(BF16)

        def head(b, carry):
            cols = pl.ds(pl.multiple_of(b * HD, HD), HD)
            w, wt, mix = head_forward(
                QKV[s, 0, :, cols], QKV[s, 1, :, cols], QKV[s, 2, :, cols], mask, scale
            )
            AW[s, b, 0:T] = w
            AW[s, b, T : 2 * T] = wt
            MIX[s, :, cols] = mix.astype(BF16)
            return carry

        lax.fori_loop(0, 8, head, 0)
        full = jnp.zeros((2 * T, 2 * R), F32)
        for ch in chunks:
            full = full + dot_nt(MIX[s, :, ch], W[s, 1, :, ch])
        put(1, *cross(full))
        total = reduce_end(1, T, reduce_start(1, T))
        m, mt = total[:, :R].astype(BF16), total[:, R:].astype(BF16)
        MS[s, 0:T] = mt
        MS[s, T : 2 * T] = m
        low = lower(m, mt)
        for ch in chunks:
            H2[s + 1, :, ch] = (
                H2[s, :, ch].astype(F32) + dot_nn(low, W[s, 5, :, ch])
            ).astype(BF16)
        return carry

    lax.fori_loop(0, 4, forward_layer, 0)

    for ch in chunks:
        for i in range(2):
            rows = slice(i * TOK, (i + 1) * TOK)
            G2[rows, ch] = (H2[4, rows, ch].astype(F32) - HY[1, i, :, ch].astype(F32)) / count
        G2[T : 2 * T, ch] = H2[4, T : 2 * T, ch].astype(F32) / count

    def backward_layer(step, carry):
        s = 3 - step
        full = jnp.zeros((2 * T, 2 * R), F32)
        for ch in chunks:
            full = full + dot_nt(G2[:, ch].astype(BF16), W[s, 5, :, ch])
        put(0, *cross(full))
        copies = reduce_start(0, T)
        for ch in chunks:
            GR[s, 5, :, ch] = dot_tn(MS[s], G2[:, ch].astype(BF16)).astype(BF16)
        total = reduce_end(0, T, copies)
        dm, dmt = total[:, :R].astype(BF16), total[:, R:].astype(BF16)
        low = lower(dm, dmt)
        swapped = jnp.concatenate([dmt, dm], 0)
        for ch in chunks:
            DMIX[:, ch] = dot_nn(low, W[s, 1, :, ch]).astype(BF16)
            GR[s, 1, :, ch] = dot_tn(swapped, MIX[s, :, ch]).astype(BF16)

        def head(b, carry):
            cols = pl.ds(pl.multiple_of(b * HD, HD), HD)
            dq, dk, dv = head_backward(
                QKV[s, 0, :, cols], QKV[s, 1, :, cols], QKV[s, 2, :, cols],
                AW[s, b, 0:T], AW[s, b, T : 2 * T], DMIX[:, cols], scale,
            )
            DX[0, :, cols] = dq.astype(BF16)
            DX[1, :, cols] = dk.astype(BF16)
            DX[2, :, cols] = dv.astype(BF16)
            return carry

        lax.fori_loop(0, 8, head, 0)
        full = jnp.zeros((2 * T, 2 * R), F32)
        for f in range(3):
            for ch in chunks:
                full = full + dot_nt(DX[f, :, ch], W[s, 2 + f, :, ch])
        put(1, *cross(full))
        copies = reduce_start(1, T)
        for f in range(3):
            for ch in chunks:
                GR[s, 2 + f, :, ch] = dot_tn(LS[s], DX[f, :, ch]).astype(BF16)
        total = reduce_end(1, T, copies)
        dl, dlt = total[:, :R], total[:, R:]
        a, at = AS[s, :, 0:R], AS[s, :, R : 2 * R]
        r, rt = RR[s, 0, :, 0:1], RR[s, 1, :, 0:1]
        dot = jnp.sum(dl * a, axis=1, keepdims=True)
        dott = jnp.sum(dlt * a + dl * at, axis=1, keepdims=True)
        kap = r * r * r * dot / D
        kapt = (3.0 * r * r * rt * dot + r * r * r * dott) / D
        low = lower((r * dl).astype(BF16), (rt * dl + r * dlt).astype(BF16))
        swapped = jnp.concatenate([dlt, dl], 0).astype(BF16)
        for ch in chunks:
            h = H2[s, 0:T, ch].astype(F32)
            ht = H2[s, T : 2 * T, ch].astype(F32)
            normed = jnp.concatenate([r * h, r * ht + rt * h], 0).astype(BF16)
            GR[s, 0, :, ch] = dot_tn(swapped, normed).astype(BF16)
            inner = dot_nn(low, W[s, 0, :, ch])
            G2[0:T, ch] = G2[0:T, ch] + inner[:T] - kap * h
            G2[T : 2 * T, ch] = G2[T : 2 * T, ch] + inner[T:] - kapt * h - kap * ht
        return carry

    lax.fori_loop(0, 4, backward_layer, 0)

    swap = []
    for i in range(2):
        swap.append(send(GR.at[2 * i + 1 - c], RB0.at[i], sa.at[i], ra.at[i], sibling))
    for i in range(2):
        swap[i].wait_recv()

        def add(f, carry):
            here = GR[2 * i + c, f].astype(F32) + RB0[i, f].astype(F32)
            GR[2 * i + c, f] = here.astype(BF16)
            return carry

        lax.fori_loop(0, 6, add, 0)

    right, left = devp(p1 + 1, p2), devp(p1 - 1, p2)
    right2, left2 = devp(p1, p2 + 1), devp(p1, p2 - 1)
    order = (2, 1, -1, 0)
    ends = []
    halves = []
    for k, o in enumerate(order):
        q2 = p2 + o
        halves.append((
            send(piece(GR, p1 + 2, q2, 0, 3), RH.at[0, k], sb.at[0, k], rb.at[0, k], right),
            send(piece(GR, p1 + 2, q2, 3, 6), RH.at[1, k], sb.at[1, k], rb.at[1, k], left),
        ))
    wholes = []
    for k, o in enumerate(order):
        q2 = p2 + o
        pair = []
        for i, d in enumerate((1, -1)):
            halves[k][i].wait_recv()
            f0, f1 = ((0, 3), (3, 6))[i]
            there = piece(GR, p1 + d, q2, f0, f1)
            there[...] = (there[...].astype(F32) + RH[i, k].astype(F32)).astype(BF16)
            pair.append(
                send(
                    piece(GR, p1 + d, q2, 0, 6), RF.at[i, k], sb.at[2 + i, k], rb.at[2 + i, k],
                    (right, left)[i],
                )
            )
        wholes.append(pair)
    second = []
    for k, o in enumerate(order):
        for i in range(2):
            wholes[k][i].wait_recv()
        here = piece(GR, p1, p2 + o, 0, 6)
        total = here[...].astype(F32) + RF[0, k].astype(F32) + RF[1, k].astype(F32)
        P1[k] = total.astype(BF16)
        if k == 0:
            second.append(send(P1.at[0, 0:3], RH2.at[0], sc.at[0], rc.at[0], right2))
            second.append(send(P1.at[0, 3:6], RH2.at[1], sc.at[1], rc.at[1], left2))
        elif k <= 2:
            i = k - 1
            f0, f1 = ((0, 3), (3, 6))[i]
            second[i].wait_recv()
            P1[k, f0:f1] = (P1[k, f0:f1].astype(F32) + RH2[i].astype(F32)).astype(BF16)
            second.append(send(P1.at[k], RF2.at[i], sc.at[2 + i], rc.at[2 + i], (right2, left2)[i]))
    second[2].wait_recv()
    second[3].wait_recv()
    down_ref[0] = P1[3, 0:2].astype(F32) + RF2[0, 0:2].astype(F32) + RF2[1, 0:2].astype(F32)
    up_ref[0] = P1[3, 2:6].astype(F32) + RF2[0, 2:6].astype(F32) + RF2[1, 2:6].astype(F32)
    for group in (sent, swap, second, *halves, *wholes):
        for copy in group:
            copy.wait_send()


def body(hidden_in, targets, down_factors, up_factors, down_dir, up_dir):
    _, TOK, D = hidden_in.shape
    R, HD = down_factors.shape[2], down_factors.shape[3]
    T, C = 2 * TOK, 8 * HD
    count = 64.0 * TOK
    which = lax.axis_index("section") // 2
    both = jnp.stack(
        [
            lax.dynamic_index_in_dim(hidden_in, which, 0, keepdims=False),
            lax.dynamic_index_in_dim(targets, which, 0, keepdims=False),
        ]
    )
    hy = both.reshape(2, TOK, 8, 4, HD).transpose(3, 0, 1, 2, 4).reshape(4, 2, TOK, C)
    dma = pltpu.SemaphoreType.DMA
    vm = pltpu.VMEM
    return pl.pallas_call(
        functools.partial(kernel, (R, HD, TOK, float(D), count)),
        out_shape=(
            jax.ShapeDtypeStruct((1, 2, R, HD), F32),
            jax.ShapeDtypeStruct((1, 4, R, HD), F32),
        ),
        in_specs=[pl.BlockSpec(memory_space=pl.ANY)] * 5,
        out_specs=(pl.BlockSpec(memory_space=vm), pl.BlockSpec(memory_space=vm)),
        scratch_shapes=[
            vm((4, 6, 2 * R, C), BF16),
            vm((2, 2, TOK, C), BF16),
            vm((5, 2 * T, C), BF16),
            vm((4, 3, 2 * T, C), BF16),
            vm((4, 8, 2 * T, T), BF16),
            vm((4, 2 * T, C), BF16),
            vm((4, T, 2 * R), F32),
            vm((4, 2, T, R), F32),
            vm((4, 2 * T, R), BF16),
            vm((4, 2 * T, R), BF16),
            vm((2 * T, C), F32),
            vm((3, 2 * T, C), BF16),
            vm((2 * T, C), BF16),
            vm((4, 6, R, C), BF16),
            vm((2, T + 16, 2 * R), BF16),
            vm((2, 3, T + 16, 2 * R), BF16),
            vm((2, 6, R, C), BF16),
            vm((2, 4, 3, R, HD), BF16),
            vm((2, 4, 6, R, HD), BF16),
            vm((4, 6, R, HD), BF16),
            vm((2, 3, R, HD), BF16),
            vm((2, 6, R, HD), BF16),
            dma((4,)),
            dma((4,)), dma((4,)),
            dma((16,)), dma((16,)),
            dma((16,)), dma((16,)),
            dma((3,)), dma((2,)),
            dma((2, 3)), dma((2, 3)),
            dma((2,)), dma((2,)),
            dma((4, 4)), dma((4, 4)),
            dma((4,)), dma((4,)),
        ],
        compiler_params=pltpu.CompilerParams(
            collective_id=0, has_side_effects=True, vmem_limit_bytes=58 * 2**20
        ),
    )(hy, down_factors, up_factors, down_dir, up_dir)


def solution(mesh):
    in_specs = (
        P("dp", None, None),
        P("dp", None, None),
        P("section", None, None, "dp"),
        P("section", None, None, "dp"),
        P("section", None, None, "dp"),
        P("section", None, None, "dp"),
    )
    out_specs = (P("section", None, None, "dp"), P("section", None, None, "dp"))
    return jax.shard_map(body, mesh=mesh, in_specs=in_specs, out_specs=out_specs, check_vma=False)
```

```python
import functools
import math

import jax
import jax.numpy as jnp
from jax import lax
from jax.experimental import pallas as pl
from jax.experimental.pallas import tpu as pltpu
from jax.sharding import PartitionSpec as P

EPS = 1e-05
MESH = pl.DeviceIdType.MESH
F32 = jnp.float32
BF16 = jnp.bfloat16


def dot_nt(a, b):
    return lax.dot_general(a, b, (((1,), (1,)), ((), ())), preferred_element_type=F32)


def dot_tn(a, b):
    return lax.dot_general(a, b, (((0,), (0,)), ((), ())), preferred_element_type=F32)


def dot_nn(a, b):
    return lax.dot_general(a, b, (((1,), (0,)), ((), ())), preferred_element_type=F32)


def lower(a, at):
    return jnp.concatenate(
        [jnp.concatenate([a, jnp.zeros_like(a)], 1), jnp.concatenate([at, a], 1)], 0
    )


def cross(full):
    n, m = full.shape[0] // 2, full.shape[1] // 2
    return full[:n, :m], full[:n, m:] + full[n:, :m]


def head_forward(q2, k2, v2, mask, scale):
    s, st = cross(dot_nt(q2, k2))
    s = jnp.where(mask, s * scale, -1e30)
    st = st * scale
    e = jnp.exp(s - jnp.max(s, axis=-1, keepdims=True))
    w = e / jnp.sum(e, axis=-1, keepdims=True)
    wt = w * (st - jnp.sum(w * st, axis=-1, keepdims=True))
    w, wt = w.astype(BF16), wt.astype(BF16)
    return w, wt, dot_nn(lower(w, wt), v2)


def head_backward(q2, k2, v2, w, wt, dm2, scale):
    n = w.shape[0]
    da, dat = cross(dot_nt(dm2, v2))
    dvs = dot_tn(lower(w, wt), jnp.concatenate([dm2[n:], dm2[:n]], 0))
    wf, wtf = w.astype(F32), wt.astype(F32)
    da = da - jnp.sum(wf * da, axis=-1, keepdims=True)
    wda = wf * da
    dst = wtf * da + wf * dat
    dst = dst - wf * jnp.sum(dst, axis=-1, keepdims=True)
    ds = (wda * scale).astype(BF16)
    dst = (dst * scale).astype(BF16)
    low = lower(ds, dst)
    dq2 = dot_nn(low, k2)
    dks = dot_tn(low, jnp.concatenate([q2[n:], q2[:n]], 0))
    return (
        dq2,
        jnp.concatenate([dks[n:], dks[:n]], 0),
        jnp.concatenate([dvs[n:], dvs[:n]], 0),
    )


def kernel(
    dims,
    hy_ref, df_ref, uf_ref, dd_ref, ud_ref,
    down_ref, up_ref,
    W, HY, H2, QKV, AW, MIX, AS, RR, MS, LS, G2, DX, DMIX, GR,
    snd, rcv, RB0, RH, RF, P1, RH2, RF2,
    own_sem, s1, r1, s2, r2, s3, r3, hs, hr, ars, arr, sa, ra, sb, rb, sc, rc,
):
    R, HD, TOK, D, count = dims
    T = 2 * TOK
    C = 8 * HD
    CH = 2 * HD
    dp = lax.axis_index("dp")
    sec = lax.axis_index("section")
    x = 2 * (sec // 2) + dp // 16
    y = (dp // 4) % 4
    z = dp % 4
    c = sec % 2

    def dev(x, y, z, c):
        return ((x % 2) * 16 + y * 4 + z, (x // 2) * 2 + c)

    def to_xy(p1, p2):
        return p1 * (1 - c) + p2 * c, p2 * (1 - c) + p1 * c

    p1 = x * (1 - c) + y * c
    p2 = y * (1 - c) + x * c

    def devp(q1, q2):
        xx, yy = to_xy(q1 % 4, q2 % 4)
        return dev(xx, yy, z, c)

    def piece(ref, q1, q2, f0, f1):
        xx, yy = to_xy(q1 % 4, q2 % 4)
        col = pl.multiple_of(((xx % 2) * 4 + yy) * HD, HD)
        return ref.at[2 * (xx // 2) + c, f0:f1, :, pl.ds(col, HD)]

    sibling = dev(x, y, z, 1 - c)

    def send(src, dst, ssem, rsem, to):
        copy = pltpu.make_async_remote_copy(
            src_ref=src, dst_ref=dst, send_sem=ssem, recv_sem=rsem,
            device_id=to, device_id_type=MESH,
        )
        copy.start()
        return copy

    mine = [
        pltpu.make_async_copy(df_ref.at[0], piece(W, p1, p2, 0, 2).at[:, 0:R], own_sem.at[0]),
        pltpu.make_async_copy(dd_ref.at[0], piece(W, p1, p2, 0, 2).at[:, R : 2 * R], own_sem.at[1]),
        pltpu.make_async_copy(uf_ref.at[0], piece(W, p1, p2, 2, 6).at[:, 0:R], own_sem.at[2]),
        pltpu.make_async_copy(ud_ref.at[0], piece(W, p1, p2, 2, 6).at[:, R : 2 * R], own_sem.at[3]),
    ]
    for copy in mine:
        copy.start()

    barrier = pltpu.get_barrier_semaphore()
    peers = [
        devp(p1 + 1, p2), devp(p1 - 1, p2), devp(p1, p2 + 1), devp(p1, p2 - 1), sibling,
        dev(x, y, (z + 1) % 4, c), dev(x, y, (z + 2) % 4, c), dev(x, y, (z + 3) % 4, c),
    ]
    for peer in peers:
        pl.semaphore_signal(barrier, inc=1, device_id=peer, device_id_type=MESH)
    pl.semaphore_wait(barrier, len(peers))

    for copy in mine:
        copy.wait()

    sent = []

    def ring_send(q1, q2, ssem, rsem, axis):
        for i, d in enumerate((1, -1)):
            to = devp(p1 + d, p2) if axis == 1 else devp(p1, p2 + d)
            sent.append(
                send(piece(W, q1, q2, 0, 6), piece(W, q1, q2, 0, 6), ssem(i), rsem(i), to)
            )

    def forward(i, q1, q2, ssem, rsem, axis):
        d = (1, -1)[i]
        to = devp(p1 + d, p2) if axis == 1 else devp(p1, p2 + d)
        f0, f1 = ((0, 3), (3, 6))[i]
        sent.append(
            send(piece(W, q1, q2, f0, f1), piece(W, q1, q2, f0, f1), ssem(2 + i), rsem(2 + i), to)
        )

    def expect(q1, q2, f0, f1, rsem):
        ref = piece(W, q1, q2, f0, f1)
        pltpu.make_async_copy(ref, ref, rsem).wait()

    def share(i, q1, q2):
        sent.append(
            send(piece(W, q1, q2, 0, 6), piece(W, q1, q2, 0, 6), s3.at[i], r3.at[i], sibling)
        )

    offs = (0, -1, 1, 2)

    def start_second(k):
        q1 = p1 + offs[k]
        ring_send(q1, p2, lambda i: s2.at[4 * k + i], lambda i: r2.at[4 * k + i], 2)
        share(4 * k, q1, p2)

    def relay_second(k):
        q1 = p1 + offs[k]
        for i, d in enumerate((-1, 1)):
            expect(q1, p2 + d, 0, 6, r2.at[4 * k + i])
            forward(i, q1, p2 + d, lambda j: s2.at[4 * k + j], lambda j: r2.at[4 * k + j], 2)
            share(4 * k + 1 + i, q1, p2 + d)

    def end_second(k):
        q1 = p1 + offs[k]
        expect(q1, p2 + 2, 0, 3, r2.at[4 * k + 2])
        expect(q1, p2 + 2, 3, 6, r2.at[4 * k + 3])
        share(4 * k + 3, q1, p2 + 2)

    ring_send(p1, p2, lambda i: s1.at[i], lambda i: r1.at[i], 1)
    start_second(0)
    half = z // 2

    @pl.when(z % 2 == c)
    def _():
        for j in range(2):
            pltpu.make_async_copy(hy_ref.at[z, j], HY.at[j, half], hr.at[j, half]).start()
            for d in (1, 2, 3):
                to = (z + d) % 4
                send(
                    hy_ref.at[to, j], HY.at[j, half], hs.at[j, d - 1], hr.at[j, half],
                    dev(x, y, to, c),
                )

    for i, d in enumerate((-1, 1)):
        expect(p1 + d, p2, 0, 6, r1.at[i])
        forward(i, p1 + d, p2, lambda j: s1.at[j], lambda j: r1.at[j], 1)
        start_second(1 + i)
    relay_second(0)
    expect(p1 + 2, p2, 0, 3, r1.at[2])
    expect(p1 + 2, p2, 3, 6, r1.at[3])
    start_second(3)
    relay_second(1)
    relay_second(2)
    end_second(0)
    relay_second(3)
    end_second(1)
    end_second(2)
    end_second(3)

    def expect_rows(j):
        for i in range(2):
            pltpu.make_async_copy(HY.at[j, i], HY.at[j, i], hr.at[j, i]).wait()

    expect_rows(0)
    for i in range(16):
        ref = piece(W, p1, p2, 0, 6)
        pltpu.make_async_copy(ref, ref, r3.at[i]).wait()

    row = lax.broadcasted_iota(jnp.int32, (T, T), 0)
    col = lax.broadcasted_iota(jnp.int32, (T, T), 1)
    eye = row == col
    mask = (row >= col) & ((row < TOK) == (col < TOK))
    scale = 1.0 / math.sqrt(HD)

    def to_row(column):
        return jnp.sum(jnp.where(eye, column, 0.0), axis=0, keepdims=True)

    def to_column(line):
        return jnp.sum(jnp.where(eye, line, 0.0), axis=1, keepdims=True)

    def reduce_start(par, rows):
        copies = []
        for d in (1, 2, 3):
            copies.append(
                send(
                    snd.at[par, 0:rows], rcv.at[par, d - 1, 0:rows],
                    ars.at[par, d - 1], arr.at[par, d - 1], dev(x, y, (z + d) % 4, c),
                )
            )
        return copies

    def reduce_end(par, rows, copies):
        for copy in copies:
            copy.wait()
        total = snd[par, 0:rows].astype(F32)
        for d in range(3):
            total = total + rcv[par, d, 0:rows].astype(F32)
        return total

    def put(par, value, tangent):
        snd[par, 0:T, 0:R] = value.astype(BF16)
        snd[par, 0:T, R : 2 * R] = tangent.astype(BF16)

    chunks = [slice(j, j + CH) for j in range(0, C, CH)]

    for i in range(2):
        H2[0, i * TOK : (i + 1) * TOK] = HY[0, i]
    H2[0, T : 2 * T] = jnp.zeros((T, C), BF16)

    def forward_layer(s, carry):
        full = jnp.zeros((2 * T, 2 * R), F32)
        ss = jnp.zeros((T, 1), F32)
        st = jnp.zeros((T, 1), F32)
        for ch in chunks:
            h2 = H2[s, :, ch]
            full = full + dot_nt(h2, W[s, 0, :, ch])
            hf = h2[:T].astype(F32)
            ss = ss + jnp.sum(hf * hf, axis=1, keepdims=True)
            st = st + jnp.sum(hf * h2[T:].astype(F32), axis=1, keepdims=True)
        put(0, *cross(full))
        line = jnp.concatenate([to_row(ss), to_row(st)], 1)
        high = line.astype(BF16).astype(F32)
        place = lax.broadcasted_iota(jnp.int32, (16, 2 * T), 0)
        pair = jnp.where(place == 0, high, jnp.where(place == 1, line - high, 0.0))
        snd[0, T : T + 16, :] = pair.astype(BF16)
        total = reduce_end(0, T + 16, reduce_start(0, T + 16))
        line = jnp.sum(total[T:], axis=0, keepdims=True)
        ss, st = to_column(line[:, :T]), to_column(line[:, T:])
        r = lax.rsqrt(ss / D + EPS)
        rt = -(r * r * r) * st / D
        a, at = total[:T, :R], total[:T, R:]
        AS[s] = total[:T]
        RR[s, 0] = jnp.broadcast_to(r, (T, R))
        RR[s, 1] = jnp.broadcast_to(rt, (T, R))
        lat = (r * a).astype(BF16)
        latt = (r * at + rt * a).astype(BF16)
        LS[s, 0:T] = latt
        LS[s, T : 2 * T] = lat
        low = lower(lat, latt)
        for f in range(3):
            for ch in chunks:
                QKV[s, f, :, ch] = dot_nn(low, W[s, 2 + f, :, ch]).astype(BF16)

        def head(b, carry):
            cols = pl.ds(pl.multiple_of(b * HD, HD), HD)
            w, wt, mix = head_forward(
                QKV[s, 0, :, cols], QKV[s, 1, :, cols], QKV[s, 2, :, cols], mask, scale
            )
            AW[s, b, 0:T] = w
            AW[s, b, T : 2 * T] = wt
            MIX[s, :, cols] = mix.astype(BF16)
            return carry

        lax.fori_loop(0, 8, head, 0, unroll=True)
        full = jnp.zeros((2 * T, 2 * R), F32)
        for ch in chunks:
            full = full + dot_nt(MIX[s, :, ch], W[s, 1, :, ch])
        put(1, *cross(full))
        total = reduce_end(1, T, reduce_start(1, T))
        m, mt = total[:, :R].astype(BF16), total[:, R:].astype(BF16)
        MS[s, 0:T] = mt
        MS[s, T : 2 * T] = m
        low = lower(m, mt)
        for ch in chunks:
            H2[s + 1, :, ch] = (
                H2[s, :, ch].astype(F32) + dot_nn(low, W[s, 5, :, ch])
            ).astype(BF16)
        return carry

    lax.fori_loop(0, 4, forward_layer, 0)
    expect_rows(1)

    for ch in chunks:
        for i in range(2):
            rows = slice(i * TOK, (i + 1) * TOK)
            G2[rows, ch] = (H2[4, rows, ch].astype(F32) - HY[1, i, :, ch].astype(F32)) / count
        G2[T : 2 * T, ch] = H2[4, T : 2 * T, ch].astype(F32) / count

    def backward_layer(step, carry):
        s = 3 - step
        full = jnp.zeros((2 * T, 2 * R), F32)
        for ch in chunks:
            full = full + dot_nt(G2[:, ch].astype(BF16), W[s, 5, :, ch])
        put(0, *cross(full))
        copies = reduce_start(0, T)
        for ch in chunks:
            GR[s, 5, :, ch] = dot_tn(MS[s], G2[:, ch].astype(BF16)).astype(BF16)
        total = reduce_end(0, T, copies)
        dm, dmt = total[:, :R].astype(BF16), total[:, R:].astype(BF16)
        low = lower(dm, dmt)
        swapped = jnp.concatenate([dmt, dm], 0)
        for ch in chunks:
            DMIX[:, ch] = dot_nn(low, W[s, 1, :, ch]).astype(BF16)
            GR[s, 1, :, ch] = dot_tn(swapped, MIX[s, :, ch]).astype(BF16)

        def head(b, carry):
            cols = pl.ds(pl.multiple_of(b * HD, HD), HD)
            dq, dk, dv = head_backward(
                QKV[s, 0, :, cols], QKV[s, 1, :, cols], QKV[s, 2, :, cols],
                AW[s, b, 0:T], AW[s, b, T : 2 * T], DMIX[:, cols], scale,
            )
            DX[0, :, cols] = dq.astype(BF16)
            DX[1, :, cols] = dk.astype(BF16)
            DX[2, :, cols] = dv.astype(BF16)
            return carry

        lax.fori_loop(0, 8, head, 0, unroll=True)
        full = jnp.zeros((2 * T, 2 * R), F32)
        for f in range(3):
            for ch in chunks:
                full = full + dot_nt(DX[f, :, ch], W[s, 2 + f, :, ch])
        put(1, *cross(full))
        copies = reduce_start(1, T)
        for f in range(3):
            for ch in chunks:
                GR[s, 2 + f, :, ch] = dot_tn(LS[s], DX[f, :, ch]).astype(BF16)
        total = reduce_end(1, T, copies)
        dl, dlt = total[:, :R], total[:, R:]
        a, at = AS[s, :, 0:R], AS[s, :, R : 2 * R]
        r, rt = RR[s, 0, :, 0:1], RR[s, 1, :, 0:1]
        dot = jnp.sum(dl * a, axis=1, keepdims=True)
        dott = jnp.sum(dlt * a + dl * at, axis=1, keepdims=True)
        kap = r * r * r * dot / D
        kapt = (3.0 * r * r * rt * dot + r * r * r * dott) / D
        low = lower((r * dl).astype(BF16), (rt * dl + r * dlt).astype(BF16))
        swapped = jnp.concatenate([dlt, dl], 0).astype(BF16)
        for ch in chunks:
            h = H2[s, 0:T, ch].astype(F32)
            ht = H2[s, T : 2 * T, ch].astype(F32)
            normed = jnp.concatenate([r * h, r * ht + rt * h], 0).astype(BF16)
            GR[s, 0, :, ch] = dot_tn(swapped, normed).astype(BF16)
            inner = dot_nn(low, W[s, 0, :, ch])
            G2[0:T, ch] = G2[0:T, ch] + inner[:T] - kap * h
            G2[T : 2 * T, ch] = G2[T : 2 * T, ch] + inner[T:] - kapt * h - kap * ht
        return carry

    lax.fori_loop(0, 4, backward_layer, 0)

    swap = []
    for i in range(2):
        swap.append(send(GR.at[2 * i + 1 - c], RB0.at[i], sa.at[i], ra.at[i], sibling))
    for i in range(2):
        swap[i].wait_recv()

        def add(f, carry):
            here = GR[2 * i + c, f].astype(F32) + RB0[i, f].astype(F32)
            GR[2 * i + c, f] = here.astype(BF16)
            return carry

        lax.fori_loop(0, 6, add, 0)

    right, left = devp(p1 + 1, p2), devp(p1 - 1, p2)
    right2, left2 = devp(p1, p2 + 1), devp(p1, p2 - 1)
    order = (2, 1, -1, 0)
    ends = []
    halves = []
    for k, o in enumerate(order):
        q2 = p2 + o
        halves.append((
            send(piece(GR, p1 + 2, q2, 0, 3), RH.at[0, k], sb.at[0, k], rb.at[0, k], right),
            send(piece(GR, p1 + 2, q2, 3, 6), RH.at[1, k], sb.at[1, k], rb.at[1, k], left),
        ))
    wholes = []
    for k, o in enumerate(order):
        q2 = p2 + o
        pair = []
        for i, d in enumerate((1, -1)):
            halves[k][i].wait_recv()
            f0, f1 = ((0, 3), (3, 6))[i]
            there = piece(GR, p1 + d, q2, f0, f1)
            there[...] = (there[...].astype(F32) + RH[i, k].astype(F32)).astype(BF16)
            pair.append(
                send(
                    piece(GR, p1 + d, q2, 0, 6), RF.at[i, k], sb.at[2 + i, k], rb.at[2 + i, k],
                    (right, left)[i],
                )
            )
        wholes.append(pair)
    second = []
    for k, o in enumerate(order):
        for i in range(2):
            wholes[k][i].wait_recv()
        here = piece(GR, p1, p2 + o, 0, 6)
        total = here[...].astype(F32) + RF[0, k].astype(F32) + RF[1, k].astype(F32)
        P1[k] = total.astype(BF16)
        if k == 0:
            second.append(send(P1.at[0, 0:3], RH2.at[0], sc.at[0], rc.at[0], right2))
            second.append(send(P1.at[0, 3:6], RH2.at[1], sc.at[1], rc.at[1], left2))
        elif k <= 2:
            i = k - 1
            f0, f1 = ((0, 3), (3, 6))[i]
            second[i].wait_recv()
            P1[k, f0:f1] = (P1[k, f0:f1].astype(F32) + RH2[i].astype(F32)).astype(BF16)
            second.append(send(P1.at[k], RF2.at[i], sc.at[2 + i], rc.at[2 + i], (right2, left2)[i]))
    second[2].wait_recv()
    second[3].wait_recv()
    down_ref[0] = P1[3, 0:2].astype(F32) + RF2[0, 0:2].astype(F32) + RF2[1, 0:2].astype(F32)
    up_ref[0] = P1[3, 2:6].astype(F32) + RF2[0, 2:6].astype(F32) + RF2[1, 2:6].astype(F32)
    @pl.when(z % 2 == c)
    def _():
        for j in range(2):
            for d in range(3):
                ref = HY.at[j, half]
                pltpu.make_async_copy(ref, ref, hs.at[j, d]).wait()

    for group in (sent, swap, second, *halves, *wholes):
        for copy in group:
            copy.wait_send()


def body(hidden_in, targets, down_factors, up_factors, down_dir, up_dir):
    _, TOK, D = hidden_in.shape
    R, HD = down_factors.shape[2], down_factors.shape[3]
    T, C = 2 * TOK, 8 * HD
    count = 64.0 * TOK
    which = lax.axis_index("section") // 2
    both = jnp.stack(
        [
            lax.dynamic_index_in_dim(hidden_in, which, 0, keepdims=False),
            lax.dynamic_index_in_dim(targets, which, 0, keepdims=False),
        ]
    )
    hy = both.reshape(2, TOK, 8, 4, HD).transpose(3, 0, 1, 2, 4).reshape(4, 2, TOK, C)
    dma = pltpu.SemaphoreType.DMA
    vm = pltpu.VMEM
    return pl.pallas_call(
        functools.partial(kernel, (R, HD, TOK, float(D), count)),
        out_shape=(
            jax.ShapeDtypeStruct((1, 2, R, HD), F32),
            jax.ShapeDtypeStruct((1, 4, R, HD), F32),
        ),
        in_specs=[pl.BlockSpec(memory_space=pl.ANY)] * 5,
        out_specs=(pl.BlockSpec(memory_space=vm), pl.BlockSpec(memory_space=vm)),
        scratch_shapes=[
            vm((4, 6, 2 * R, C), BF16),
            vm((2, 2, TOK, C), BF16),
            vm((5, 2 * T, C), BF16),
            vm((4, 3, 2 * T, C), BF16),
            vm((4, 8, 2 * T, T), BF16),
            vm((4, 2 * T, C), BF16),
            vm((4, T, 2 * R), F32),
            vm((4, 2, T, R), F32),
            vm((4, 2 * T, R), BF16),
            vm((4, 2 * T, R), BF16),
            vm((2 * T, C), F32),
            vm((3, 2 * T, C), BF16),
            vm((2 * T, C), BF16),
            vm((4, 6, R, C), BF16),
            vm((2, T + 16, 2 * R), BF16),
            vm((2, 3, T + 16, 2 * R), BF16),
            vm((2, 6, R, C), BF16),
            vm((2, 4, 3, R, HD), BF16),
            vm((2, 4, 6, R, HD), BF16),
            vm((4, 6, R, HD), BF16),
            vm((2, 3, R, HD), BF16),
            vm((2, 6, R, HD), BF16),
            dma((4,)),
            dma((4,)), dma((4,)),
            dma((16,)), dma((16,)),
            dma((16,)), dma((16,)),
            dma((2, 3)), dma((2, 2)),
            dma((2, 3)), dma((2, 3)),
            dma((2,)), dma((2,)),
            dma((4, 4)), dma((4, 4)),
            dma((4,)), dma((4,)),
        ],
        compiler_params=pltpu.CompilerParams(
            collective_id=0, has_side_effects=True, vmem_limit_bytes=58 * 2**20
        ),
    )(hy, down_factors, up_factors, down_dir, up_dir)


def solution(mesh):
    in_specs = (
        P("dp", None, None),
        P("dp", None, None),
        P("section", None, None, "dp"),
        P("section", None, None, "dp"),
        P("section", None, None, "dp"),
        P("section", None, None, "dp"),
    )
    out_specs = (P("section", None, None, "dp"), P("section", None, None, "dp"))
    return jax.shard_map(body, mesh=mesh, in_specs=in_specs, out_specs=out_specs, check_vma=False)
```

```python
import functools
import math

import jax
import jax.numpy as jnp
from jax import lax
from jax.experimental import pallas as pl
from jax.experimental.pallas import tpu as pltpu
from jax.sharding import PartitionSpec as P

EPS = 1e-05
MESH = pl.DeviceIdType.MESH
F32 = jnp.float32
BF16 = jnp.bfloat16


def dot_nt(a, b):
    return lax.dot_general(a, b, (((1,), (1,)), ((), ())), preferred_element_type=F32)


def dot_tn(a, b):
    return lax.dot_general(a, b, (((0,), (0,)), ((), ())), preferred_element_type=F32)


def dot_nn(a, b):
    return lax.dot_general(a, b, (((1,), (0,)), ((), ())), preferred_element_type=F32)


def lower(a, at):
    return jnp.concatenate(
        [jnp.concatenate([a, jnp.zeros_like(a)], 1), jnp.concatenate([at, a], 1)], 0
    )


def cross(full):
    n, m = full.shape[0] // 2, full.shape[1] // 2
    return full[:n, :m], full[:n, m:] + full[n:, :m]


def head_forward(q2, k2, v2, mask, scale):
    s, st = cross(dot_nt(q2, k2))
    s = jnp.where(mask, s * scale, -1e30)
    st = st * scale
    e = jnp.exp(s - jnp.max(s, axis=-1, keepdims=True))
    w = e / jnp.sum(e, axis=-1, keepdims=True)
    wt = w * (st - jnp.sum(w * st, axis=-1, keepdims=True))
    w, wt = w.astype(BF16), wt.astype(BF16)
    return w, wt, dot_nn(lower(w, wt), v2)


def head_backward(q2, k2, v2, w, wt, dm2, scale):
    n = w.shape[0]
    da, dat = cross(dot_nt(dm2, v2))
    dvs = dot_tn(lower(w, wt), jnp.concatenate([dm2[n:], dm2[:n]], 0))
    wf, wtf = w.astype(F32), wt.astype(F32)
    da = da - jnp.sum(wf * da, axis=-1, keepdims=True)
    wda = wf * da
    dst = wtf * da + wf * dat
    dst = dst - wf * jnp.sum(dst, axis=-1, keepdims=True)
    ds = (wda * scale).astype(BF16)
    dst = (dst * scale).astype(BF16)
    low = lower(ds, dst)
    dq2 = dot_nn(low, k2)
    dks = dot_tn(low, jnp.concatenate([q2[n:], q2[:n]], 0))
    return (
        dq2,
        jnp.concatenate([dks[n:], dks[:n]], 0),
        jnp.concatenate([dvs[n:], dvs[:n]], 0),
    )


def kernel(
    dims,
    hy_ref, df_ref, uf_ref, dd_ref, ud_ref,
    down_ref, up_ref,
    W, HY, H2, QKV, AW, MIX, AS, RR, MS, LS, G2, DX, DMIX, GR,
    SS, FS, GP, GV, GA, ZE, DMB, bgs, bgr, bs, br, gs, gv, gt, ga, gx,
    snd, rcv, RB0, RH, RF, P1, RH2, RF2,
    own_sem, s1, r1, s2, r2, s3, r3, hs, hr, ars, arr, sa, ra, sb, rb, sc, rc,
):
    R, HD, TOK, D, count = dims
    T = 2 * TOK
    C = 8 * HD
    CH = 2 * HD
    dp = lax.axis_index("dp")
    sec = lax.axis_index("section")
    x = 2 * (sec // 2) + dp // 16
    y = (dp // 4) % 4
    z = dp % 4
    c = sec % 2

    def dev(x, y, z, c):
        return ((x % 2) * 16 + y * 4 + z, (x // 2) * 2 + c)

    def to_xy(p1, p2):
        return p1 * (1 - c) + p2 * c, p2 * (1 - c) + p1 * c

    p1 = x * (1 - c) + y * c
    p2 = y * (1 - c) + x * c

    def devp(q1, q2):
        xx, yy = to_xy(q1 % 4, q2 % 4)
        return dev(xx, yy, z, c)

    def piece(ref, q1, q2, f0, f1):
        xx, yy = to_xy(q1 % 4, q2 % 4)
        col = pl.multiple_of(((xx % 2) * 4 + yy) * HD, HD)
        return ref.at[2 * (xx // 2) + c, f0:f1, :, pl.ds(col, HD)]

    sibling = dev(x, y, z, 1 - c)

    def send(src, dst, ssem, rsem, to):
        copy = pltpu.make_async_remote_copy(
            src_ref=src, dst_ref=dst, send_sem=ssem, recv_sem=rsem,
            device_id=to, device_id_type=MESH,
        )
        copy.start()
        return copy

    mine = [
        pltpu.make_async_copy(df_ref.at[0], piece(W, p1, p2, 0, 2).at[:, 0:R], own_sem.at[0]),
        pltpu.make_async_copy(dd_ref.at[0], piece(W, p1, p2, 0, 2).at[:, R : 2 * R], own_sem.at[1]),
        pltpu.make_async_copy(uf_ref.at[0], piece(W, p1, p2, 2, 6).at[:, 0:R], own_sem.at[2]),
        pltpu.make_async_copy(ud_ref.at[0], piece(W, p1, p2, 2, 6).at[:, R : 2 * R], own_sem.at[3]),
    ]
    for copy in mine:
        copy.start()

    barrier = pltpu.get_barrier_semaphore()
    peers = [
        devp(p1 + 1, p2), devp(p1 - 1, p2), devp(p1, p2 + 1), devp(p1, p2 - 1), sibling,
        dev(x, y, (z + 1) % 4, c), dev(x, y, (z + 2) % 4, c), dev(x, y, (z + 3) % 4, c),
    ]
    for peer in peers:
        pl.semaphore_signal(barrier, inc=1, device_id=peer, device_id_type=MESH)
    pl.semaphore_wait(barrier, len(peers))

    for copy in mine:
        copy.wait()

    sent = []

    def ring_send(q1, q2, ssem, rsem, axis):
        for i, d in enumerate((1, -1)):
            to = devp(p1 + d, p2) if axis == 1 else devp(p1, p2 + d)
            sent.append(
                send(piece(W, q1, q2, 0, 6), piece(W, q1, q2, 0, 6), ssem(i), rsem(i), to)
            )

    def forward(i, q1, q2, ssem, rsem, axis):
        d = (1, -1)[i]
        to = devp(p1 + d, p2) if axis == 1 else devp(p1, p2 + d)
        f0, f1 = ((0, 3), (3, 6))[i]
        sent.append(
            send(piece(W, q1, q2, f0, f1), piece(W, q1, q2, f0, f1), ssem(2 + i), rsem(2 + i), to)
        )

    def expect(q1, q2, f0, f1, rsem):
        ref = piece(W, q1, q2, f0, f1)
        pltpu.make_async_copy(ref, ref, rsem).wait()

    def share(i, q1, q2):
        sent.append(
            send(piece(W, q1, q2, 0, 6), piece(W, q1, q2, 0, 6), s3.at[i], r3.at[i], sibling)
        )

    offs = (0, -1, 1, 2)

    def start_second(k):
        q1 = p1 + offs[k]
        ring_send(q1, p2, lambda i: s2.at[4 * k + i], lambda i: r2.at[4 * k + i], 2)
        share(4 * k, q1, p2)

    def relay_second(k):
        q1 = p1 + offs[k]
        for i, d in enumerate((-1, 1)):
            expect(q1, p2 + d, 0, 6, r2.at[4 * k + i])
            forward(i, q1, p2 + d, lambda j: s2.at[4 * k + j], lambda j: r2.at[4 * k + j], 2)
            share(4 * k + 1 + i, q1, p2 + d)

    def end_second(k):
        q1 = p1 + offs[k]
        expect(q1, p2 + 2, 0, 3, r2.at[4 * k + 2])
        expect(q1, p2 + 2, 3, 6, r2.at[4 * k + 3])
        share(4 * k + 3, q1, p2 + 2)

    ring_send(p1, p2, lambda i: s1.at[i], lambda i: r1.at[i], 1)
    start_second(0)
    half = z // 2

    @pl.when(z % 2 == c)
    def _():
        for j in range(2):
            pltpu.make_async_copy(hy_ref.at[z, j], HY.at[j, half], hr.at[j, half]).start()
            for d in (1, 2, 3):
                to = (z + d) % 4
                send(
                    hy_ref.at[to, j], HY.at[j, half], hs.at[j, d - 1], hr.at[j, half],
                    dev(x, y, to, c),
                )

    for i, d in enumerate((-1, 1)):
        expect(p1 + d, p2, 0, 6, r1.at[i])
        forward(i, p1 + d, p2, lambda j: s1.at[j], lambda j: r1.at[j], 1)
        start_second(1 + i)
    relay_second(0)
    expect(p1 + 2, p2, 0, 3, r1.at[2])
    expect(p1 + 2, p2, 3, 6, r1.at[3])
    start_second(3)
    relay_second(1)
    relay_second(2)
    end_second(0)
    relay_second(3)
    end_second(1)
    end_second(2)
    end_second(3)

    def expect_rows(j):
        for i in range(2):
            pltpu.make_async_copy(HY.at[j, i], HY.at[j, i], hr.at[j, i]).wait()

    expect_rows(0)
    for i in range(16):
        ref = piece(W, p1, p2, 0, 6)
        pltpu.make_async_copy(ref, ref, r3.at[i]).wait()

    row = lax.broadcasted_iota(jnp.int32, (T, T), 0)
    col = lax.broadcasted_iota(jnp.int32, (T, T), 1)
    eye = row == col
    mask = (row >= col) & ((row < TOK) == (col < TOK))
    scale = 1.0 / math.sqrt(HD)

    def to_row(column):
        return jnp.sum(jnp.where(eye, column, 0.0), axis=0, keepdims=True)

    def to_column(line):
        return jnp.sum(jnp.where(eye, line, 0.0), axis=1, keepdims=True)

    def reduce_start(par, rows):
        copies = []
        for d in (1, 2, 3):
            copies.append(
                send(
                    snd.at[par, 0:rows], rcv.at[par, d - 1, 0:rows],
                    ars.at[par, d - 1], arr.at[par, d - 1], dev(x, y, (z + d) % 4, c),
                )
            )
        return copies

    def reduce_end(par, rows, copies):
        for copy in copies:
            copy.wait()
        total = snd[par, 0:rows].astype(F32)
        for d in range(3):
            total = total + rcv[par, d, 0:rows].astype(F32)
        return total

    def put(par, value, tangent):
        snd[par, 0:T, 0:R] = value.astype(BF16)
        snd[par, 0:T, R : 2 * R] = tangent.astype(BF16)

    chunks = [slice(j, j + CH) for j in range(0, C, CH)]

    def when(condition):
        return (lambda run: run()) if condition else (lambda run: None)

    def products(left, right):
        full = jnp.zeros((2 * T, 2 * R), F32)
        for ch in chunks:
            full = full + dot_nt(left(ch), right(ch))
        return cross(full)

    def later(par, width):
        return [
            pltpu.make_async_remote_copy(
                src_ref=bgs.at[par, :, 0:width], dst_ref=bgr.at[par, d - 1, :, 0:width],
                send_sem=bs.at[par, d - 1], recv_sem=br.at[par, d - 1],
                device_id=dev(x, y, (z + d) % 4, c), device_id_type=MESH,
            )
            for d in (1, 2, 3)
        ]

    def put_later(par, i, pair):
        bgs[par, :, 2 * i * R : (2 * i + 1) * R] = pair[0].astype(BF16)
        bgs[par, :, (2 * i + 1) * R : (2 * i + 2) * R] = pair[1].astype(BF16)

    def sum_later(par, i):
        cols = slice(2 * i * R, (2 * i + 2) * R)
        total = bgs[par, :, cols].astype(F32)
        for d in range(3):
            total = total + bgr[par, d, :, cols].astype(F32)
        return total

    for i in range(2):
        H2[0, i * TOK : (i + 1) * TOK] = HY[0, i]
    H2[0, T : 2 * T] = jnp.zeros((T, C), BF16)

    put(0, *products(lambda ch: H2[0, :, ch], lambda ch: W[0, 0, :, ch]))
    ss = jnp.zeros((T, 1), F32)
    for ch in chunks:
        hf = H2[0, 0:T, ch].astype(F32)
        ss = ss + jnp.sum(hf * hf, axis=1, keepdims=True)
    line = to_row(ss)
    high = line.astype(BF16).astype(F32)
    place = lax.broadcasted_iota(jnp.int32, (16, T), 0)
    pair = jnp.where(place == 0, high, jnp.where(place == 1, line - high, 0.0))
    snd[0, T : T + 16, 0:T] = pair.astype(BF16)
    snd[0, T : T + 16, T : 2 * T] = jnp.zeros((16, T), BF16)
    copies = reduce_start(0, T + 16)

    HR = R // 2
    RQ = R // 8
    first = pl.multiple_of(c * HR, HR)

    def own(s, right):
        full = jnp.zeros((2 * HR, 2 * R), F32)
        for ch in chunks:
            left = jnp.concatenate(
                [W[s, 5, pl.ds(first, HR), ch], W[s, 5, pl.ds(R + first, HR), ch]], 0
            )
            full = full + dot_nt(left, right(ch))
        return cross(full)

    for i in range(7):
        j = i % 4
        if i < 4:
            pair = own(j, lambda ch: W[j, 5, :, ch])
        else:
            pair = own(j, lambda ch: W[j + 1, 0, :, ch])
        for k in range(2):
            GP[:, (2 * i + k) * R : (2 * i + k + 1) * R] = pair[k].astype(BF16)

    def quarter(ref, zz):
        return ref.at[pl.ds(pl.multiple_of((zz % 4) * RQ, RQ), RQ)]

    gram_in, gram_out = [], []
    for d in (1, 2, 3):
        to = dev(x, y, (z + d) % 4, c)
        gram_in.append(
            send(quarter(GP, z + d), GV.at[d - 1], gs.at[d - 1], gv.at[d - 1], to)
        )
        gram_out.append(
            pltpu.make_async_remote_copy(
                src_ref=quarter(GA.at[c], z), dst_ref=quarter(GA.at[c], z),
                send_sem=gt.at[d - 1], recv_sem=ga.at[d - 1],
                device_id=to, device_id_type=MESH,
            )
        )
    gram_share = pltpu.make_async_remote_copy(
        src_ref=GA.at[c], dst_ref=GA.at[c], send_sem=gx.at[0], recv_sem=gx.at[1],
        device_id=sibling, device_id_type=MESH,
    )

    def gram_sum():
        total = quarter(GP, z)[...].astype(F32)
        for copy in gram_in:
            copy.wait()
        for d in range(3):
            total = total + GV[d].astype(F32)
        quarter(GA.at[c], z)[...] = total.astype(BF16)
        for copy in gram_out:
            copy.start()

    def gram_pass():
        for copy in gram_out:
            copy.wait()
        gram_share.start()

    def gram(i):
        cols = [slice((2 * i + k) * R, (2 * i + k + 1) * R) for k in range(2)]
        return jnp.concatenate([GA[h, :, cols[k]] for k in range(2) for h in range(2)], 0)

    expect_rows(1)
    for i in range(2):
        H2[5, i * TOK : (i + 1) * TOK] = HY[1, i]
    H2[5, T : 2 * T] = jnp.zeros((T, C), BF16)
    total = reduce_end(0, T + 16, copies)
    AS[0] = total[:T]
    SS[0] = jnp.broadcast_to(to_column(jnp.sum(total[T:, 0:T], axis=0, keepdims=True)), (T, R))
    SS[1] = jnp.zeros((T, R), F32)

    def forward_layer(s, carry):
        par = s % 2
        slot = (1 + s) % 2
        last = int(s == 3)
        lhs, layer, factor = s + 2 * last, s + 1 - last, 5 * last
        put_later(par, 0, products(lambda ch: H2[lhs, :, ch], lambda ch: W[layer, factor, :, ch]))
        put_later(par, 1, products(lambda ch: H2[s, :, ch], lambda ch: W[s, 5, :, ch]))
        others = later(par, 4 * R)
        for copy in others:
            copy.start()
        ss, st = SS[0, :, 0:1], SS[1, :, 0:1]
        r = lax.rsqrt(ss / D + EPS)
        rt = -(r * r * r) * st / D
        a, at = AS[s, :, 0:R], AS[s, :, R : 2 * R]
        RR[s, 0] = jnp.broadcast_to(r, (T, R))
        RR[s, 1] = jnp.broadcast_to(rt, (T, R))
        lat = (r * a).astype(BF16)
        latt = (r * at + rt * a).astype(BF16)
        LS[s, 0:T] = latt
        LS[s, T : 2 * T] = lat
        low = lower(lat, latt)
        for f in range(3):
            for ch in chunks:
                QKV[s, f, :, ch] = dot_nn(low, W[s, 2 + f, :, ch]).astype(BF16)

        if s == 0:
            gram_sum()

        def head(b, carry):
            cols = pl.ds(pl.multiple_of(b * HD, HD), HD)
            w, wt, mix = head_forward(
                QKV[s, 0, :, cols], QKV[s, 1, :, cols], QKV[s, 2, :, cols], mask, scale
            )
            AW[s, b, 0:T] = w
            AW[s, b, T : 2 * T] = wt
            MIX[s, :, cols] = mix.astype(BF16)
            return carry

        lax.fori_loop(0, 8, head, 0, unroll=True)
        put(slot, *products(lambda ch: MIX[s, :, ch], lambda ch: W[s, 1, :, ch]))
        copies = reduce_start(slot, T)
        if s == 0:
            gram_pass()
        for copy in others:
            copy.wait()
        ZE[:, 0 : 2 * R] = sum_later(par, 0)
        ZE[:, 2 * R : 4 * R] = sum_later(par, 1)
        total = reduce_end(slot, T, copies)
        m, mt = total[:, :R].astype(BF16), total[:, R:].astype(BF16)
        MS[s, 0:T] = mt
        MS[s, T : 2 * T] = m
        low = lower(m, mt)
        for ch in chunks:
            H2[s + 1, :, ch] = (
                H2[s, :, ch].astype(F32) + dot_nn(low, W[s, 5, :, ch])
            ).astype(BF16)
        if s == 0:
            gram_share.wait()
        if s < 3:
            add = dot_nn(low, gram(4 + s))
            AS[s + 1, :, 0:R] = ZE[:, 0:R] + add[:T]
            AS[s + 1, :, R : 2 * R] = ZE[:, R : 2 * R] + add[T:]
        k = dot_nn(low, gram(s))
        k, kt = k[:T], k[T:]
        e, et = ZE[:, 2 * R : 3 * R], ZE[:, 3 * R : 4 * R]
        FS[s, :, 0:R] = e + k
        FS[s, :, R : 2 * R] = et + kt
        m, mt = m.astype(F32), mt.astype(F32)
        ss = ss + jnp.sum(m * (2.0 * e + k), axis=1, keepdims=True)
        st = st + jnp.sum(mt * e + m * et + 0.5 * (mt * k + m * kt), axis=1, keepdims=True)
        SS[0] = jnp.broadcast_to(ss, (T, R))
        SS[1] = jnp.broadcast_to(st, (T, R))
        return carry

    for s in range(4):
        forward_layer(s, 0)

    DMB[0:T] = ((FS[3, :, R : 2 * R] - ZE[:, R : 2 * R]) / count).astype(BF16)
    DMB[T : 2 * T] = ((FS[3, :, 0:R] - ZE[:, 0:R]) / count).astype(BF16)
    for ch in chunks:
        G2[0:T, ch] = (H2[4, 0:T, ch].astype(F32) - H2[5, 0:T, ch].astype(F32)) / count
        G2[T : 2 * T, ch] = H2[4, T : 2 * T, ch].astype(F32) / count

    def backward_layer(step, carry):
        s = 3 - step
        par = step % 2
        slot = (1 + step) % 2
        others = later(par, 2 * R) if s > 0 else []

        @when(s > 0)
        def _():
            put_later(
                par, 0, products(lambda ch: G2[:, ch].astype(BF16), lambda ch: W[s - 1, 5, :, ch])
            )
            for copy in others:
                copy.start()

        low = lower(DMB[T : 2 * T], DMB[0:T])
        for ch in chunks:
            DMIX[:, ch] = dot_nn(low, W[s, 1, :, ch]).astype(BF16)

        def head(b, carry):
            cols = pl.ds(pl.multiple_of(b * HD, HD), HD)
            dq, dk, dv = head_backward(
                QKV[s, 0, :, cols], QKV[s, 1, :, cols], QKV[s, 2, :, cols],
                AW[s, b, 0:T], AW[s, b, T : 2 * T], DMIX[:, cols], scale,
            )
            DX[0, :, cols] = dq.astype(BF16)
            DX[1, :, cols] = dk.astype(BF16)
            DX[2, :, cols] = dv.astype(BF16)
            return carry

        lax.fori_loop(0, 8, head, 0, unroll=True)
        full = jnp.zeros((2 * T, 2 * R), F32)
        for f in range(3):
            for ch in chunks:
                full = full + dot_nt(DX[f, :, ch], W[s, 2 + f, :, ch])
        put(slot, *cross(full))
        copies = reduce_start(slot, T)
        for ch in chunks:
            GR[s, 5, :, ch] = dot_tn(MS[s], G2[:, ch].astype(BF16)).astype(BF16)
            GR[s, 1, :, ch] = dot_tn(DMB[...], MIX[s, :, ch]).astype(BF16)
        for f in range(3):
            for ch in chunks:
                GR[s, 2 + f, :, ch] = dot_tn(LS[s], DX[f, :, ch]).astype(BF16)

        @when(s > 0)
        def _():
            for copy in others:
                copy.wait()
            ZE[:, 0 : 2 * R] = sum_later(par, 0)

        total = reduce_end(slot, T, copies)
        dl, dlt = total[:, :R], total[:, R:]
        a, at = AS[s, :, 0:R], AS[s, :, R : 2 * R]
        r, rt = RR[s, 0, :, 0:1], RR[s, 1, :, 0:1]
        dot = jnp.sum(dl * a, axis=1, keepdims=True)
        dott = jnp.sum(dlt * a + dl * at, axis=1, keepdims=True)
        kap = r * r * r * dot / D
        kapt = (3.0 * r * r * rt * dot + r * r * r * dott) / D
        rl, rlt = (r * dl).astype(BF16), (rt * dl + r * dlt).astype(BF16)
        swapped = jnp.concatenate([dlt, dl], 0).astype(BF16)

        @when(s > 0)
        def _():
            v, t = cross(dot_nt(jnp.concatenate([rl, rlt], 0), gram(3 + s)))
            f, ft = FS[s - 1, :, 0:R], FS[s - 1, :, R : 2 * R]
            DMB[0:T] = (ZE[:, R : 2 * R] + t - kapt * f - kap * ft).astype(BF16)
            DMB[T : 2 * T] = (ZE[:, 0:R] + v - kap * f).astype(BF16)
            low = lower(rl, rlt)
            for ch in chunks:
                h = H2[s, 0:T, ch].astype(F32)
                ht = H2[s, T : 2 * T, ch].astype(F32)
                inner = dot_nn(low, W[s, 0, :, ch])
                G2[0:T, ch] = G2[0:T, ch] + inner[:T] - kap * h
                G2[T : 2 * T, ch] = G2[T : 2 * T, ch] + inner[T:] - kapt * h - kap * ht

        for ch in chunks:
            h = H2[s, 0:T, ch].astype(F32)
            ht = H2[s, T : 2 * T, ch].astype(F32)
            normed = jnp.concatenate([r * h, r * ht + rt * h], 0).astype(BF16)
            GR[s, 0, :, ch] = dot_tn(swapped, normed).astype(BF16)
        return carry

    for step in range(4):
        backward_layer(step, 0)

    swap = []
    for i in range(2):
        swap.append(send(GR.at[2 * i + 1 - c], RB0.at[i], sa.at[i], ra.at[i], sibling))
    for i in range(2):
        swap[i].wait_recv()

        def add(f, carry):
            here = GR[2 * i + c, f].astype(F32) + RB0[i, f].astype(F32)
            GR[2 * i + c, f] = here.astype(BF16)
            return carry

        lax.fori_loop(0, 6, add, 0)

    right, left = devp(p1 + 1, p2), devp(p1 - 1, p2)
    right2, left2 = devp(p1, p2 + 1), devp(p1, p2 - 1)
    order = (2, 1, -1, 0)
    ends = []
    halves = []
    for k, o in enumerate(order):
        q2 = p2 + o
        halves.append((
            send(piece(GR, p1 + 2, q2, 0, 3), RH.at[0, k], sb.at[0, k], rb.at[0, k], right),
            send(piece(GR, p1 + 2, q2, 3, 6), RH.at[1, k], sb.at[1, k], rb.at[1, k], left),
        ))
    wholes = []
    for k, o in enumerate(order):
        q2 = p2 + o
        pair = []
        for i, d in enumerate((1, -1)):
            halves[k][i].wait_recv()
            f0, f1 = ((0, 3), (3, 6))[i]
            there = piece(GR, p1 + d, q2, f0, f1)
            there[...] = (there[...].astype(F32) + RH[i, k].astype(F32)).astype(BF16)
            pair.append(
                send(
                    piece(GR, p1 + d, q2, 0, 6), RF.at[i, k], sb.at[2 + i, k], rb.at[2 + i, k],
                    (right, left)[i],
                )
            )
        wholes.append(pair)
    second = []
    for k, o in enumerate(order):
        for i in range(2):
            wholes[k][i].wait_recv()
        here = piece(GR, p1, p2 + o, 0, 6)
        total = here[...].astype(F32) + RF[0, k].astype(F32) + RF[1, k].astype(F32)
        P1[k] = total.astype(BF16)
        if k == 0:
            second.append(send(P1.at[0, 0:3], RH2.at[0], sc.at[0], rc.at[0], right2))
            second.append(send(P1.at[0, 3:6], RH2.at[1], sc.at[1], rc.at[1], left2))
        elif k <= 2:
            i = k - 1
            f0, f1 = ((0, 3), (3, 6))[i]
            second[i].wait_recv()
            P1[k, f0:f1] = (P1[k, f0:f1].astype(F32) + RH2[i].astype(F32)).astype(BF16)
            second.append(send(P1.at[k], RF2.at[i], sc.at[2 + i], rc.at[2 + i], (right2, left2)[i]))
    second[2].wait_recv()
    second[3].wait_recv()
    down_ref[0] = P1[3, 0:2].astype(F32) + RF2[0, 0:2].astype(F32) + RF2[1, 0:2].astype(F32)
    up_ref[0] = P1[3, 2:6].astype(F32) + RF2[0, 2:6].astype(F32) + RF2[1, 2:6].astype(F32)
    @pl.when(z % 2 == c)
    def _():
        for j in range(2):
            for d in range(3):
                ref = HY.at[j, half]
                pltpu.make_async_copy(ref, ref, hs.at[j, d]).wait()

    for group in (sent, swap, second, *halves, *wholes):
        for copy in group:
            copy.wait_send()


def body(hidden_in, targets, down_factors, up_factors, down_dir, up_dir):
    _, TOK, D = hidden_in.shape
    R, HD = down_factors.shape[2], down_factors.shape[3]
    T, C = 2 * TOK, 8 * HD
    count = 64.0 * TOK
    which = lax.axis_index("section") // 2
    both = jnp.stack(
        [
            lax.dynamic_index_in_dim(hidden_in, which, 0, keepdims=False),
            lax.dynamic_index_in_dim(targets, which, 0, keepdims=False),
        ]
    )
    hy = both.reshape(2, TOK, 8, 4, HD).transpose(3, 0, 1, 2, 4).reshape(4, 2, TOK, C)
    dma = pltpu.SemaphoreType.DMA
    vm = pltpu.VMEM
    return pl.pallas_call(
        functools.partial(kernel, (R, HD, TOK, float(D), count)),
        out_shape=(
            jax.ShapeDtypeStruct((1, 2, R, HD), F32),
            jax.ShapeDtypeStruct((1, 4, R, HD), F32),
        ),
        in_specs=[pl.BlockSpec(memory_space=pl.ANY)] * 5,
        out_specs=(pl.BlockSpec(memory_space=vm), pl.BlockSpec(memory_space=vm)),
        scratch_shapes=[
            vm((4, 6, 2 * R, C), BF16),
            vm((2, 2, TOK, C), BF16),
            vm((6, 2 * T, C), BF16),
            vm((4, 3, 2 * T, C), BF16),
            vm((4, 8, 2 * T, T), BF16),
            vm((4, 2 * T, C), BF16),
            vm((4, T, 2 * R), F32),
            vm((4, 2, T, R), F32),
            vm((4, 2 * T, R), BF16),
            vm((4, 2 * T, R), BF16),
            vm((2 * T, C), F32),
            vm((3, 2 * T, C), BF16),
            vm((2 * T, C), BF16),
            vm((4, 6, R, C), BF16),
            vm((2, T, R), F32),
            vm((4, T, 2 * R), F32),
            vm((R // 2, 14 * R), BF16),
            vm((3, R // 8, 14 * R), BF16),
            vm((2, R // 2, 14 * R), BF16),
            vm((T, 4 * R), F32),
            vm((2 * T, R), BF16),
            vm((2, T, 4 * R), BF16),
            vm((2, 3, T, 4 * R), BF16),
            dma((2, 3)), dma((2, 3)),
            dma((3,)), dma((3,)), dma((3,)), dma((3,)), dma((2,)),
            vm((2, T + 16, 2 * R), BF16),
            vm((2, 3, T + 16, 2 * R), BF16),
            vm((2, 6, R, C), BF16),
            vm((2, 4, 3, R, HD), BF16),
            vm((2, 4, 6, R, HD), BF16),
            vm((4, 6, R, HD), BF16),
            vm((2, 3, R, HD), BF16),
            vm((2, 6, R, HD), BF16),
            dma((4,)),
            dma((4,)), dma((4,)),
            dma((16,)), dma((16,)),
            dma((16,)), dma((16,)),
            dma((2, 3)), dma((2, 2)),
            dma((2, 3)), dma((2, 3)),
            dma((2,)), dma((2,)),
            dma((4, 4)), dma((4, 4)),
            dma((4,)), dma((4,)),
        ],
        compiler_params=pltpu.CompilerParams(
            collective_id=0, has_side_effects=True, vmem_limit_bytes=58 * 2**20
        ),
    )(hy, down_factors, up_factors, down_dir, up_dir)


def solution(mesh):
    in_specs = (
        P("dp", None, None),
        P("dp", None, None),
        P("section", None, None, "dp"),
        P("section", None, None, "dp"),
        P("section", None, None, "dp"),
        P("section", None, None, "dp"),
    )
    out_specs = (P("section", None, None, "dp"), P("section", None, None, "dp"))
    return jax.shard_map(body, mesh=mesh, in_specs=in_specs, out_specs=out_specs, check_vma=False)
```

```python
import functools
import math

import jax
import jax.numpy as jnp
from jax import lax
from jax.experimental import pallas as pl
from jax.experimental.pallas import tpu as pltpu
from jax.sharding import PartitionSpec as P

EPS = 1e-05
MESH = pl.DeviceIdType.MESH
F32 = jnp.float32
BF16 = jnp.bfloat16


def dot_nt(a, b):
    return lax.dot_general(a, b, (((1,), (1,)), ((), ())), preferred_element_type=F32)


def dot_tn(a, b):
    return lax.dot_general(a, b, (((0,), (0,)), ((), ())), preferred_element_type=F32)


def dot_nn(a, b):
    return lax.dot_general(a, b, (((1,), (0,)), ((), ())), preferred_element_type=F32)


def lower(a, at):
    return jnp.concatenate(
        [jnp.concatenate([a, jnp.zeros_like(a)], 1), jnp.concatenate([at, a], 1)], 0
    )


def cross(full):
    n, m = full.shape[0] // 2, full.shape[1] // 2
    return full[:n, :m], full[:n, m:] + full[n:, :m]


def head_forward(q2, k2, v2, mask, scale):
    s, st = cross(dot_nt(q2, k2))
    s = jnp.where(mask, s * scale, -1e30)
    st = st * scale
    e = jnp.exp(s - jnp.max(s, axis=-1, keepdims=True))
    w = e / jnp.sum(e, axis=-1, keepdims=True)
    wt = w * (st - jnp.sum(w * st, axis=-1, keepdims=True))
    w, wt = w.astype(BF16), wt.astype(BF16)
    return w, wt, dot_nn(lower(w, wt), v2)


def head_backward(q2, k2, v2, w, wt, dm2, scale):
    n = w.shape[0]
    da, dat = cross(dot_nt(dm2, v2))
    dvs = dot_tn(lower(w, wt), jnp.concatenate([dm2[n:], dm2[:n]], 0))
    wf, wtf = w.astype(F32), wt.astype(F32)
    da = da - jnp.sum(wf * da, axis=-1, keepdims=True)
    wda = wf * da
    dst = wtf * da + wf * dat
    dst = dst - wf * jnp.sum(dst, axis=-1, keepdims=True)
    ds = (wda * scale).astype(BF16)
    dst = (dst * scale).astype(BF16)
    low = lower(ds, dst)
    dq2 = dot_nn(low, k2)
    dks = dot_tn(low, jnp.concatenate([q2[n:], q2[:n]], 0))
    return (
        dq2,
        jnp.concatenate([dks[n:], dks[:n]], 0),
        jnp.concatenate([dvs[n:], dvs[:n]], 0),
    )


def kernel(
    dims,
    hid_ref, tar_ref, df_ref, uf_ref, dd_ref, ud_ref,
    out_ref,
    W, HY, H2, QKV, AW, MIX, AS, RR, MS, LS, G2, DX, DMIX, GR,
    SS, FS, GP, GV, GA, ZE, DMB, bgs, bgr, bs, br, gs, gv, gt, ga, gx,
    snd, rcv, RB0, RH, RF, P1, RH2, RF2,
    own_sem, s1, r1, s2, r2, s3, r3, hs, hr, ars, arr, sa, ra, sb, rb, sc, rc,
):
    R, HD, TOK, D, count = dims
    T = 2 * TOK
    C = 8 * HD
    CH = 2 * HD
    dp = lax.axis_index("dp")
    sec = lax.axis_index("section")
    x = 2 * (sec // 2) + dp // 16
    y = (dp // 4) % 4
    z = dp % 4
    c = sec % 2

    def dev(x, y, z, c):
        return ((x % 2) * 16 + y * 4 + z, (x // 2) * 2 + c)

    def to_xy(p1, p2):
        return p1 * (1 - c) + p2 * c, p2 * (1 - c) + p1 * c

    p1 = x * (1 - c) + y * c
    p2 = y * (1 - c) + x * c

    def devp(q1, q2):
        xx, yy = to_xy(q1 % 4, q2 % 4)
        return dev(xx, yy, z, c)

    def piece(ref, q1, q2, f0, f1):
        xx, yy = to_xy(q1 % 4, q2 % 4)
        col = pl.multiple_of(((xx % 2) * 4 + yy) * HD, HD)
        return ref.at[2 * (xx // 2) + c, f0:f1, :, pl.ds(col, HD)]

    sibling = dev(x, y, z, 1 - c)

    def send(src, dst, ssem, rsem, to):
        copy = pltpu.make_async_remote_copy(
            src_ref=src, dst_ref=dst, send_sem=ssem, recv_sem=rsem,
            device_id=to, device_id_type=MESH,
        )
        copy.start()
        return copy

    mine = [
        pltpu.make_async_copy(df_ref.at[0], piece(W, p1, p2, 0, 2).at[:, 0:R], own_sem.at[0]),
        pltpu.make_async_copy(dd_ref.at[0], piece(W, p1, p2, 0, 2).at[:, R : 2 * R], own_sem.at[1]),
        pltpu.make_async_copy(uf_ref.at[0], piece(W, p1, p2, 2, 6).at[:, 0:R], own_sem.at[2]),
        pltpu.make_async_copy(ud_ref.at[0], piece(W, p1, p2, 2, 6).at[:, R : 2 * R], own_sem.at[3]),
    ]
    for copy in mine:
        copy.start()

    barrier = pltpu.get_barrier_semaphore()
    peers = [
        devp(p1 + 1, p2), devp(p1 - 1, p2), devp(p1, p2 + 1), devp(p1, p2 - 1), sibling,
        dev(x, y, (z + 1) % 4, c), dev(x, y, (z + 2) % 4, c), dev(x, y, (z + 3) % 4, c),
    ]
    for peer in peers:
        pl.semaphore_signal(barrier, inc=1, device_id=peer, device_id_type=MESH)
    pl.semaphore_wait(barrier, len(peers))

    for copy in mine:
        copy.wait()

    sent = []

    def ring_send(q1, q2, ssem, rsem, axis):
        for i, d in enumerate((1, -1)):
            to = devp(p1 + d, p2) if axis == 1 else devp(p1, p2 + d)
            sent.append(
                send(piece(W, q1, q2, 0, 6), piece(W, q1, q2, 0, 6), ssem(i), rsem(i), to)
            )

    def forward(i, q1, q2, ssem, rsem, axis):
        d = (1, -1)[i]
        to = devp(p1 + d, p2) if axis == 1 else devp(p1, p2 + d)
        f0, f1 = ((0, 3), (3, 6))[i]
        sent.append(
            send(piece(W, q1, q2, f0, f1), piece(W, q1, q2, f0, f1), ssem(2 + i), rsem(2 + i), to)
        )

    def expect(q1, q2, f0, f1, rsem):
        ref = piece(W, q1, q2, f0, f1)
        pltpu.make_async_copy(ref, ref, rsem).wait()

    def share(i, q1, q2):
        sent.append(
            send(piece(W, q1, q2, 0, 6), piece(W, q1, q2, 0, 6), s3.at[i], r3.at[i], sibling)
        )

    offs = (0, -1, 1, 2)

    def start_second(k):
        q1 = p1 + offs[k]
        ring_send(q1, p2, lambda i: s2.at[4 * k + i], lambda i: r2.at[4 * k + i], 2)
        share(4 * k, q1, p2)

    def relay_second(k):
        q1 = p1 + offs[k]
        for i, d in enumerate((-1, 1)):
            expect(q1, p2 + d, 0, 6, r2.at[4 * k + i])
            forward(i, q1, p2 + d, lambda j: s2.at[4 * k + j], lambda j: r2.at[4 * k + j], 2)
            share(4 * k + 1 + i, q1, p2 + d)

    def end_second(k):
        q1 = p1 + offs[k]
        expect(q1, p2 + 2, 0, 3, r2.at[4 * k + 2])
        expect(q1, p2 + 2, 3, 6, r2.at[4 * k + 3])
        share(4 * k + 3, q1, p2 + 2)

    ring_send(p1, p2, lambda i: s1.at[i], lambda i: r1.at[i], 1)
    start_second(0)
    half = z // 2

    @pl.when(z % 2 == c)
    def _():
        which = x // 2
        for j, ref in enumerate((hid_ref, tar_ref)):

            def column(b, carry):
                cols = pl.ds(pl.multiple_of(b * HD, HD), HD)

                def block(zz):
                    at = pl.multiple_of((b * 4 + zz) * HD, HD)
                    return ref.at[which, :, pl.ds(at, HD)]

                into = HY.at[j, half, :, cols]
                for d in (1, 2, 3):
                    to = (z + d) % 4
                    send(block(to), into, hs.at[j, d - 1], hr.at[j, half], dev(x, y, to, c))
                pltpu.make_async_copy(block(z), into, hr.at[j, half]).start()
                return carry

            lax.fori_loop(0, 8, column, 0)

    for i, d in enumerate((-1, 1)):
        expect(p1 + d, p2, 0, 6, r1.at[i])
        forward(i, p1 + d, p2, lambda j: s1.at[j], lambda j: r1.at[j], 1)
        start_second(1 + i)
    relay_second(0)
    expect(p1 + 2, p2, 0, 3, r1.at[2])
    expect(p1 + 2, p2, 3, 6, r1.at[3])
    start_second(3)
    relay_second(1)
    relay_second(2)
    end_second(0)
    relay_second(3)
    end_second(1)
    end_second(2)
    end_second(3)

    def expect_rows(j):
        for i in range(2):
            pltpu.make_async_copy(HY.at[j, i], HY.at[j, i], hr.at[j, i]).wait()

    expect_rows(0)
    for i in range(16):
        ref = piece(W, p1, p2, 0, 6)
        pltpu.make_async_copy(ref, ref, r3.at[i]).wait()

    row = lax.broadcasted_iota(jnp.int32, (T, T), 0)
    col = lax.broadcasted_iota(jnp.int32, (T, T), 1)
    eye = row == col
    mask = (row >= col) & ((row < TOK) == (col < TOK))
    scale = 1.0 / math.sqrt(HD)

    def to_row(column):
        return jnp.sum(jnp.where(eye, column, 0.0), axis=0, keepdims=True)

    def to_column(line):
        return jnp.sum(jnp.where(eye, line, 0.0), axis=1, keepdims=True)

    def reduce_start(par, rows):
        copies = []
        for d in (1, 2, 3):
            copies.append(
                send(
                    snd.at[par, 0:rows], rcv.at[par, d - 1, 0:rows],
                    ars.at[par, d - 1], arr.at[par, d - 1], dev(x, y, (z + d) % 4, c),
                )
            )
        return copies

    def reduce_end(par, rows, copies):
        for copy in copies:
            copy.wait()
        total = snd[par, 0:rows].astype(F32)
        for d in range(3):
            total = total + rcv[par, d, 0:rows].astype(F32)
        return total

    def put(par, value, tangent):
        snd[par, 0:T, 0:R] = value.astype(BF16)
        snd[par, 0:T, R : 2 * R] = tangent.astype(BF16)

    chunks = [slice(j, j + CH) for j in range(0, C, CH)]

    def when(condition):
        return (lambda run: run()) if condition else (lambda run: None)

    def products(left, right):
        full = jnp.zeros((2 * T, 2 * R), F32)
        for ch in chunks:
            full = full + dot_nt(left(ch), right(ch))
        return cross(full)

    def later(par, width):
        return [
            pltpu.make_async_remote_copy(
                src_ref=bgs.at[par, :, 0:width], dst_ref=bgr.at[par, d - 1, :, 0:width],
                send_sem=bs.at[par, d - 1], recv_sem=br.at[par, d - 1],
                device_id=dev(x, y, (z + d) % 4, c), device_id_type=MESH,
            )
            for d in (1, 2, 3)
        ]

    def put_later(par, i, pair):
        bgs[par, :, 2 * i * R : (2 * i + 1) * R] = pair[0].astype(BF16)
        bgs[par, :, (2 * i + 1) * R : (2 * i + 2) * R] = pair[1].astype(BF16)

    def sum_later(par, i):
        cols = slice(2 * i * R, (2 * i + 2) * R)
        total = bgs[par, :, cols].astype(F32)
        for d in range(3):
            total = total + bgr[par, d, :, cols].astype(F32)
        return total

    for i in range(2):
        H2[0, i * TOK : (i + 1) * TOK] = HY[0, i]
    H2[0, T : 2 * T] = jnp.zeros((T, C), BF16)

    put(0, *products(lambda ch: H2[0, :, ch], lambda ch: W[0, 0, :, ch]))
    ss = jnp.zeros((T, 1), F32)
    for ch in chunks:
        hf = H2[0, 0:T, ch].astype(F32)
        ss = ss + jnp.sum(hf * hf, axis=1, keepdims=True)
    line = to_row(ss)
    high = line.astype(BF16).astype(F32)
    place = lax.broadcasted_iota(jnp.int32, (16, T), 0)
    pair = jnp.where(place == 0, high, jnp.where(place == 1, line - high, 0.0))
    snd[0, T : T + 16, 0:T] = pair.astype(BF16)
    snd[0, T : T + 16, T : 2 * T] = jnp.zeros((16, T), BF16)
    copies = reduce_start(0, T + 16)

    HR = R // 2
    RQ = R // 8
    first = pl.multiple_of(c * HR, HR)

    def own(s, right):
        full = jnp.zeros((2 * HR, 2 * R), F32)
        for ch in chunks:
            left = jnp.concatenate(
                [W[s, 5, pl.ds(first, HR), ch], W[s, 5, pl.ds(R + first, HR), ch]], 0
            )
            full = full + dot_nt(left, right(ch))
        return cross(full)

    for i in range(7):
        j = i % 4
        if i < 4:
            pair = own(j, lambda ch: W[j, 5, :, ch])
        else:
            pair = own(j, lambda ch: W[j + 1, 0, :, ch])
        for k in range(2):
            GP[:, (2 * i + k) * R : (2 * i + k + 1) * R] = pair[k].astype(BF16)

    def quarter(ref, zz):
        return ref.at[pl.ds(pl.multiple_of((zz % 4) * RQ, RQ), RQ)]

    gram_in, gram_out = [], []
    for d in (1, 2, 3):
        to = dev(x, y, (z + d) % 4, c)
        gram_in.append(
            send(quarter(GP, z + d), GV.at[d - 1], gs.at[d - 1], gv.at[d - 1], to)
        )
        gram_out.append(
            pltpu.make_async_remote_copy(
                src_ref=quarter(GA.at[c], z), dst_ref=quarter(GA.at[c], z),
                send_sem=gt.at[d - 1], recv_sem=ga.at[d - 1],
                device_id=to, device_id_type=MESH,
            )
        )
    gram_share = pltpu.make_async_remote_copy(
        src_ref=GA.at[c], dst_ref=GA.at[c], send_sem=gx.at[0], recv_sem=gx.at[1],
        device_id=sibling, device_id_type=MESH,
    )

    def gram_sum():
        total = quarter(GP, z)[...].astype(F32)
        for copy in gram_in:
            copy.wait()
        for d in range(3):
            total = total + GV[d].astype(F32)
        quarter(GA.at[c], z)[...] = total.astype(BF16)
        for copy in gram_out:
            copy.start()

    def gram_pass():
        for copy in gram_out:
            copy.wait()
        gram_share.start()

    def gram(i):
        cols = [slice((2 * i + k) * R, (2 * i + k + 1) * R) for k in range(2)]
        return jnp.concatenate([GA[h, :, cols[k]] for k in range(2) for h in range(2)], 0)

    expect_rows(1)
    for i in range(2):
        H2[5, i * TOK : (i + 1) * TOK] = HY[1, i]
    H2[5, T : 2 * T] = jnp.zeros((T, C), BF16)
    total = reduce_end(0, T + 16, copies)
    AS[0] = total[:T]
    SS[0] = jnp.broadcast_to(to_column(jnp.sum(total[T:, 0:T], axis=0, keepdims=True)), (T, R))
    SS[1] = jnp.zeros((T, R), F32)

    def forward_layer(s, carry):
        par = s % 2
        slot = (1 + s) % 2
        last = int(s == 3)
        lhs, layer, factor = s + 2 * last, s + 1 - last, 5 * last
        put_later(par, 0, products(lambda ch: H2[lhs, :, ch], lambda ch: W[layer, factor, :, ch]))
        put_later(par, 1, products(lambda ch: H2[s, :, ch], lambda ch: W[s, 5, :, ch]))
        others = later(par, 4 * R)
        for copy in others:
            copy.start()
        ss, st = SS[0, :, 0:1], SS[1, :, 0:1]
        r = lax.rsqrt(ss / D + EPS)
        rt = -(r * r * r) * st / D
        a, at = AS[s, :, 0:R], AS[s, :, R : 2 * R]
        RR[s, 0] = jnp.broadcast_to(r, (T, R))
        RR[s, 1] = jnp.broadcast_to(rt, (T, R))
        lat = (r * a).astype(BF16)
        latt = (r * at + rt * a).astype(BF16)
        LS[s, 0:T] = latt
        LS[s, T : 2 * T] = lat
        low = lower(lat, latt)
        for f in range(3):
            for ch in chunks:
                QKV[s, f, :, ch] = dot_nn(low, W[s, 2 + f, :, ch]).astype(BF16)

        if s == 0:
            gram_sum()

        def head(b, carry):
            cols = pl.ds(pl.multiple_of(b * HD, HD), HD)
            w, wt, mix = head_forward(
                QKV[s, 0, :, cols], QKV[s, 1, :, cols], QKV[s, 2, :, cols], mask, scale
            )
            AW[s, b, 0:T] = w
            AW[s, b, T : 2 * T] = wt
            MIX[s, :, cols] = mix.astype(BF16)
            return carry

        lax.fori_loop(0, 8, head, 0, unroll=True)
        put(slot, *products(lambda ch: MIX[s, :, ch], lambda ch: W[s, 1, :, ch]))
        copies = reduce_start(slot, T)
        if s == 0:
            gram_pass()
        for copy in others:
            copy.wait()
        ZE[:, 0 : 2 * R] = sum_later(par, 0)
        ZE[:, 2 * R : 4 * R] = sum_later(par, 1)
        total = reduce_end(slot, T, copies)
        m, mt = total[:, :R].astype(BF16), total[:, R:].astype(BF16)
        MS[s, 0:T] = mt
        MS[s, T : 2 * T] = m
        low = lower(m, mt)
        for ch in chunks:
            H2[s + 1, :, ch] = (
                H2[s, :, ch].astype(F32) + dot_nn(low, W[s, 5, :, ch])
            ).astype(BF16)
        if s == 0:
            gram_share.wait()
        if s < 3:
            add = dot_nn(low, gram(4 + s))
            AS[s + 1, :, 0:R] = ZE[:, 0:R] + add[:T]
            AS[s + 1, :, R : 2 * R] = ZE[:, R : 2 * R] + add[T:]
        k = dot_nn(low, gram(s))
        k, kt = k[:T], k[T:]
        e, et = ZE[:, 2 * R : 3 * R], ZE[:, 3 * R : 4 * R]
        FS[s, :, 0:R] = e + k
        FS[s, :, R : 2 * R] = et + kt
        m, mt = m.astype(F32), mt.astype(F32)
        ss = ss + jnp.sum(m * (2.0 * e + k), axis=1, keepdims=True)
        st = st + jnp.sum(mt * e + m * et + 0.5 * (mt * k + m * kt), axis=1, keepdims=True)
        SS[0] = jnp.broadcast_to(ss, (T, R))
        SS[1] = jnp.broadcast_to(st, (T, R))
        return carry

    for s in range(4):
        forward_layer(s, 0)

    DMB[0:T] = ((FS[3, :, R : 2 * R] - ZE[:, R : 2 * R]) / count).astype(BF16)
    DMB[T : 2 * T] = ((FS[3, :, 0:R] - ZE[:, 0:R]) / count).astype(BF16)
    for ch in chunks:
        G2[0:T, ch] = (H2[4, 0:T, ch].astype(F32) - H2[5, 0:T, ch].astype(F32)) / count
        G2[T : 2 * T, ch] = H2[4, T : 2 * T, ch].astype(F32) / count

    def give(s, f0, f1, i):
        @pl.when(c != s % 2)
        def _():
            send(
                GR.at[s, f0:f1], RB0.at[s // 2, f0:f1], sa.at[s // 2, i], ra.at[s // 2, i], sibling
            )

    def add_other(hi):
        for i, (f0, f1) in enumerate(((1, 6), (0, 1))):
            ref = RB0.at[hi, f0:f1]
            pltpu.make_async_copy(ref, ref, ra.at[hi, i]).wait()

        def add(f, carry):
            here = GR[2 * hi + c, f].astype(F32) + RB0[hi, f].astype(F32)
            GR[2 * hi + c, f] = here.astype(BF16)
            return carry

        lax.fori_loop(0, 6, add, 0)

    def backward_layer(step, carry):
        s = 3 - step
        par = step % 2
        slot = (1 + step) % 2
        others = later(par, 2 * R) if s > 0 else []

        @when(s > 0)
        def _():
            put_later(
                par, 0, products(lambda ch: G2[:, ch].astype(BF16), lambda ch: W[s - 1, 5, :, ch])
            )
            for copy in others:
                copy.start()

        low = lower(DMB[T : 2 * T], DMB[0:T])
        for ch in chunks:
            DMIX[:, ch] = dot_nn(low, W[s, 1, :, ch]).astype(BF16)

        def head(b, carry):
            cols = pl.ds(pl.multiple_of(b * HD, HD), HD)
            dq, dk, dv = head_backward(
                QKV[s, 0, :, cols], QKV[s, 1, :, cols], QKV[s, 2, :, cols],
                AW[s, b, 0:T], AW[s, b, T : 2 * T], DMIX[:, cols], scale,
            )
            DX[0, :, cols] = dq.astype(BF16)
            DX[1, :, cols] = dk.astype(BF16)
            DX[2, :, cols] = dv.astype(BF16)
            return carry

        lax.fori_loop(0, 8, head, 0, unroll=True)
        full = jnp.zeros((2 * T, 2 * R), F32)
        for f in range(3):
            for ch in chunks:
                full = full + dot_nt(DX[f, :, ch], W[s, 2 + f, :, ch])
        put(slot, *cross(full))
        copies = reduce_start(slot, T)
        for ch in chunks:
            GR[s, 5, :, ch] = dot_tn(MS[s], G2[:, ch].astype(BF16)).astype(BF16)
            GR[s, 1, :, ch] = dot_tn(DMB[...], MIX[s, :, ch]).astype(BF16)
        for f in range(3):
            for ch in chunks:
                GR[s, 2 + f, :, ch] = dot_tn(LS[s], DX[f, :, ch]).astype(BF16)
        give(s, 1, 6, 0)
        if s == 0:
            add_other(1)

        @when(s > 0)
        def _():
            for copy in others:
                copy.wait()
            ZE[:, 0 : 2 * R] = sum_later(par, 0)

        total = reduce_end(slot, T, copies)
        dl, dlt = total[:, :R], total[:, R:]
        a, at = AS[s, :, 0:R], AS[s, :, R : 2 * R]
        r, rt = RR[s, 0, :, 0:1], RR[s, 1, :, 0:1]
        dot = jnp.sum(dl * a, axis=1, keepdims=True)
        dott = jnp.sum(dlt * a + dl * at, axis=1, keepdims=True)
        kap = r * r * r * dot / D
        kapt = (3.0 * r * r * rt * dot + r * r * r * dott) / D
        rl, rlt = (r * dl).astype(BF16), (rt * dl + r * dlt).astype(BF16)
        swapped = jnp.concatenate([dlt, dl], 0).astype(BF16)

        @when(s > 0)
        def _():
            v, t = cross(dot_nt(jnp.concatenate([rl, rlt], 0), gram(3 + s)))
            f, ft = FS[s - 1, :, 0:R], FS[s - 1, :, R : 2 * R]
            DMB[0:T] = (ZE[:, R : 2 * R] + t - kapt * f - kap * ft).astype(BF16)
            DMB[T : 2 * T] = (ZE[:, 0:R] + v - kap * f).astype(BF16)
            low = lower(rl, rlt)
            for ch in chunks:
                h = H2[s, 0:T, ch].astype(F32)
                ht = H2[s, T : 2 * T, ch].astype(F32)
                inner = dot_nn(low, W[s, 0, :, ch])
                G2[0:T, ch] = G2[0:T, ch] + inner[:T] - kap * h
                G2[T : 2 * T, ch] = G2[T : 2 * T, ch] + inner[T:] - kapt * h - kap * ht

        for ch in chunks:
            h = H2[s, 0:T, ch].astype(F32)
            ht = H2[s, T : 2 * T, ch].astype(F32)
            normed = jnp.concatenate([r * h, r * ht + rt * h], 0).astype(BF16)
            GR[s, 0, :, ch] = dot_tn(swapped, normed).astype(BF16)
        give(s, 0, 1, 1)
        return carry

    for step in range(4):
        backward_layer(step, 0)

    add_other(0)

    right, left = devp(p1 + 1, p2), devp(p1 - 1, p2)
    right2, left2 = devp(p1, p2 + 1), devp(p1, p2 - 1)
    order = (2, 1, -1, 0)
    ends = []
    halves = []
    for k, o in enumerate(order):
        q2 = p2 + o
        halves.append((
            send(piece(GR, p1 + 2, q2, 0, 3), RH.at[0, k], sb.at[0, k], rb.at[0, k], right),
            send(piece(GR, p1 + 2, q2, 3, 6), RH.at[1, k], sb.at[1, k], rb.at[1, k], left),
        ))
    wholes = []
    for k, o in enumerate(order):
        q2 = p2 + o
        pair = []
        for i, d in enumerate((1, -1)):
            halves[k][i].wait_recv()
            f0, f1 = ((0, 3), (3, 6))[i]
            there = piece(GR, p1 + d, q2, f0, f1)
            there[...] = (there[...].astype(F32) + RH[i, k].astype(F32)).astype(BF16)
            pair.append(
                send(
                    piece(GR, p1 + d, q2, 0, 6), RF.at[i, k], sb.at[2 + i, k], rb.at[2 + i, k],
                    (right, left)[i],
                )
            )
        wholes.append(pair)
    second = []
    for k, o in enumerate(order):
        for i in range(2):
            wholes[k][i].wait_recv()
        here = piece(GR, p1, p2 + o, 0, 6)
        total = here[...].astype(F32) + RF[0, k].astype(F32) + RF[1, k].astype(F32)
        P1[k] = total.astype(BF16)
        if k == 0:
            second.append(send(P1.at[0, 0:3], RH2.at[0], sc.at[0], rc.at[0], right2))
            second.append(send(P1.at[0, 3:6], RH2.at[1], sc.at[1], rc.at[1], left2))
        elif k <= 2:
            i = k - 1
            f0, f1 = ((0, 3), (3, 6))[i]
            second[i].wait_recv()
            P1[k, f0:f1] = (P1[k, f0:f1].astype(F32) + RH2[i].astype(F32)).astype(BF16)
            second.append(send(P1.at[k], RF2.at[i], sc.at[2 + i], rc.at[2 + i], (right2, left2)[i]))
    second[2].wait_recv()
    second[3].wait_recv()
    total = P1[3].astype(F32) + RF2[0].astype(F32) + RF2[1].astype(F32)
    out_ref[...] = total.astype(BF16)
    @pl.when(z % 2 == c)
    def _():
        for j in range(2):
            for d in range(3):
                ref = HY.at[j, half]
                pltpu.make_async_copy(ref, ref, hs.at[j, d]).wait()

    for hi in range(2):
        for i, (f0, f1) in enumerate(((1, 6), (0, 1))):
            ref = RB0.at[hi, f0:f1]
            pltpu.make_async_copy(ref, ref, sa.at[hi, i]).wait()

    for group in (sent, second, *halves, *wholes):
        for copy in group:
            copy.wait_send()


def body(hidden_in, targets, down_factors, up_factors, down_dir, up_dir):
    _, TOK, D = hidden_in.shape
    R, HD = down_factors.shape[2], down_factors.shape[3]
    T, C = 2 * TOK, 8 * HD
    count = 64.0 * TOK
    dma = pltpu.SemaphoreType.DMA
    vm = pltpu.VMEM
    out = pl.pallas_call(
        functools.partial(kernel, (R, HD, TOK, float(D), count)),
        out_shape=jax.ShapeDtypeStruct((6, R, HD), BF16),
        in_specs=[pl.BlockSpec(memory_space=pl.ANY)] * 6,
        out_specs=pl.BlockSpec(memory_space=vm),
        scratch_shapes=[
            vm((4, 6, 2 * R, C), BF16),
            vm((2, 2, TOK, C), BF16),
            vm((6, 2 * T, C), BF16),
            vm((4, 3, 2 * T, C), BF16),
            vm((4, 8, 2 * T, T), BF16),
            vm((4, 2 * T, C), BF16),
            vm((4, T, 2 * R), F32),
            vm((4, 2, T, R), F32),
            vm((4, 2 * T, R), BF16),
            vm((4, 2 * T, R), BF16),
            vm((2 * T, C), F32),
            vm((3, 2 * T, C), BF16),
            vm((2 * T, C), BF16),
            vm((4, 6, R, C), BF16),
            vm((2, T, R), F32),
            vm((4, T, 2 * R), F32),
            vm((R // 2, 14 * R), BF16),
            vm((3, R // 8, 14 * R), BF16),
            vm((2, R // 2, 14 * R), BF16),
            vm((T, 4 * R), F32),
            vm((2 * T, R), BF16),
            vm((2, T, 4 * R), BF16),
            vm((2, 3, T, 4 * R), BF16),
            dma((2, 3)), dma((2, 3)),
            dma((3,)), dma((3,)), dma((3,)), dma((3,)), dma((2,)),
            vm((2, T + 16, 2 * R), BF16),
            vm((2, 3, T + 16, 2 * R), BF16),
            vm((2, 6, R, C), BF16),
            vm((2, 4, 3, R, HD), BF16),
            vm((2, 4, 6, R, HD), BF16),
            vm((4, 6, R, HD), BF16),
            vm((2, 3, R, HD), BF16),
            vm((2, 6, R, HD), BF16),
            dma((4,)),
            dma((4,)), dma((4,)),
            dma((16,)), dma((16,)),
            dma((16,)), dma((16,)),
            dma((2, 3)), dma((2, 2)),
            dma((2, 3)), dma((2, 3)),
            dma((2, 2)), dma((2, 2)),
            dma((4, 4)), dma((4, 4)),
            dma((4,)), dma((4,)),
        ],
        compiler_params=pltpu.CompilerParams(
            collective_id=0, has_side_effects=True, vmem_limit_bytes=58 * 2**20
        ),
    )(hidden_in, targets, down_factors, up_factors, down_dir, up_dir)
    wide = out.astype(F32)
    return wide[None, 0:2], wide[None, 2:6]


def solution(mesh):
    in_specs = (
        P("dp", None, None),
        P("dp", None, None),
        P("section", None, None, "dp"),
        P("section", None, None, "dp"),
        P("section", None, None, "dp"),
        P("section", None, None, "dp"),
    )
    out_specs = (P("section", None, None, "dp"), P("section", None, None, "dp"))
    return jax.shard_map(body, mesh=mesh, in_specs=in_specs, out_specs=out_specs, check_vma=False)
```

```python
import functools
import math

import jax
import jax.numpy as jnp
from jax import lax
from jax.experimental import pallas as pl
from jax.experimental.pallas import tpu as pltpu
from jax.sharding import PartitionSpec as P

EPS = 1e-05
MESH = pl.DeviceIdType.MESH
F32 = jnp.float32
BF16 = jnp.bfloat16


def dot_nt(a, b):
    return lax.dot_general(a, b, (((1,), (1,)), ((), ())), preferred_element_type=F32)


def dot_tn(a, b):
    return lax.dot_general(a, b, (((0,), (0,)), ((), ())), preferred_element_type=F32)


def dot_nn(a, b):
    return lax.dot_general(a, b, (((1,), (0,)), ((), ())), preferred_element_type=F32)


def lower(a, at):
    return jnp.concatenate(
        [jnp.concatenate([a, jnp.zeros_like(a)], 1), jnp.concatenate([at, a], 1)], 0
    )


def cross(full):
    n, m = full.shape[0] // 2, full.shape[1] // 2
    return full[:n, :m], full[:n, m:] + full[n:, :m]


def head_forward(q2, k2, v2, mask, scale):
    s, st = cross(dot_nt(q2, k2))
    s = jnp.where(mask, s * scale, -1e30)
    st = st * scale
    e = jnp.exp(s - jnp.max(s, axis=-1, keepdims=True))
    w = e / jnp.sum(e, axis=-1, keepdims=True)
    wt = w * (st - jnp.sum(w * st, axis=-1, keepdims=True))
    w, wt = w.astype(BF16), wt.astype(BF16)
    return w, wt, dot_nn(lower(w, wt), v2)


def head_backward(q2, k2, v2, w, wt, dm2, scale):
    n = w.shape[0]
    da, dat = cross(dot_nt(dm2, v2))
    dvs = dot_tn(lower(w, wt), jnp.concatenate([dm2[n:], dm2[:n]], 0))
    wf, wtf = w.astype(F32), wt.astype(F32)
    da = da - jnp.sum(wf * da, axis=-1, keepdims=True)
    wda = wf * da
    dst = wtf * da + wf * dat
    dst = dst - wf * jnp.sum(dst, axis=-1, keepdims=True)
    ds = (wda * scale).astype(BF16)
    dst = (dst * scale).astype(BF16)
    low = lower(ds, dst)
    dq2 = dot_nn(low, k2)
    dks = dot_tn(low, jnp.concatenate([q2[n:], q2[:n]], 0))
    return (
        dq2,
        jnp.concatenate([dks[n:], dks[:n]], 0),
        jnp.concatenate([dvs[n:], dvs[:n]], 0),
    )


def kernel(
    dims,
    hid_ref, tar_ref, df_ref, uf_ref, dd_ref, ud_ref,
    out_ref,
    W, HY, H2, QKV, AW, MIX, AS, RR, MS, LS, G2, DX, DMIX, GR,
    SS, FS, GP, GV, GA, ZE, DMB, bgs, bgr, bs, br, gs, gv, gt, ga, gx,
    snd, rcv, RB0, RH, RF, P1, RH2, RF2,
    own_sem, s1, r1, s2, r2, s3, r3, hs, hr, ars, arr, sa, ra, sb, rb, sc, rc,
):
    R, HD, TOK, D, count = dims
    T = 2 * TOK
    C = 8 * HD
    CH = 2 * HD
    dp = lax.axis_index("dp")
    sec = lax.axis_index("section")
    x = 2 * (sec // 2) + dp // 16
    y = (dp // 4) % 4
    z = dp % 4
    c = sec % 2

    def dev(x, y, z, c):
        return ((x % 2) * 16 + y * 4 + z, (x // 2) * 2 + c)

    def to_xy(p1, p2):
        return p1 * (1 - c) + p2 * c, p2 * (1 - c) + p1 * c

    p1 = x * (1 - c) + y * c
    p2 = y * (1 - c) + x * c

    def devp(q1, q2):
        xx, yy = to_xy(q1 % 4, q2 % 4)
        return dev(xx, yy, z, c)

    def piece(ref, q1, q2, f0, f1):
        xx, yy = to_xy(q1 % 4, q2 % 4)
        col = pl.multiple_of(((xx % 2) * 4 + yy) * HD, HD)
        return ref.at[2 * (xx // 2) + c, f0:f1, :, pl.ds(col, HD)]

    sibling = dev(x, y, z, 1 - c)

    def send(src, dst, ssem, rsem, to):
        copy = pltpu.make_async_remote_copy(
            src_ref=src, dst_ref=dst, send_sem=ssem, recv_sem=rsem,
            device_id=to, device_id_type=MESH,
        )
        copy.start()
        return copy

    mine = [
        pltpu.make_async_copy(df_ref.at[0], piece(W, p1, p2, 0, 2).at[:, 0:R], own_sem.at[0]),
        pltpu.make_async_copy(dd_ref.at[0], piece(W, p1, p2, 0, 2).at[:, R : 2 * R], own_sem.at[1]),
        pltpu.make_async_copy(uf_ref.at[0], piece(W, p1, p2, 2, 6).at[:, 0:R], own_sem.at[2]),
        pltpu.make_async_copy(ud_ref.at[0], piece(W, p1, p2, 2, 6).at[:, R : 2 * R], own_sem.at[3]),
    ]
    for copy in mine:
        copy.start()

    barrier = pltpu.get_barrier_semaphore()
    peers = [
        devp(p1 + 1, p2), devp(p1 - 1, p2), devp(p1, p2 + 1), devp(p1, p2 - 1), sibling,
        dev(x, y, (z + 1) % 4, c), dev(x, y, (z + 2) % 4, c), dev(x, y, (z + 3) % 4, c),
    ]
    for peer in peers:
        pl.semaphore_signal(barrier, inc=1, device_id=peer, device_id_type=MESH)
    pl.semaphore_wait(barrier, len(peers))

    for copy in mine:
        copy.wait()


    def ring_send(q1, q2, ssem, rsem, axis):
        for i, d in enumerate((1, -1)):
            to = devp(p1 + d, p2) if axis == 1 else devp(p1, p2 + d)
            send(piece(W, q1, q2, 0, 6), piece(W, q1, q2, 0, 6), ssem(i), rsem(i), to)

    def forward(i, q1, q2, ssem, rsem, axis):
        d = (1, -1)[i]
        to = devp(p1 + d, p2) if axis == 1 else devp(p1, p2 + d)
        f0, f1 = ((0, 3), (3, 6))[i]
        send(piece(W, q1, q2, f0, f1), piece(W, q1, q2, f0, f1), ssem(2 + i), rsem(2 + i), to)

    def expect(q1, q2, f0, f1, rsem):
        ref = piece(W, q1, q2, f0, f1)
        pltpu.make_async_copy(ref, ref, rsem).wait()

    def share(i, q1, q2):
        send(piece(W, q1, q2, 0, 6), piece(W, q1, q2, 0, 6), s3.at[i], r3.at[i], sibling)

    offs = (0, -1, 1, 2)

    def start_second(k):
        q1 = p1 + offs[k]
        ring_send(q1, p2, lambda i: s2.at[4 * k + i], lambda i: r2.at[4 * k + i], 2)
        share(4 * k, q1, p2)

    def relay_second(k):
        q1 = p1 + offs[k]
        for i, d in enumerate((-1, 1)):
            expect(q1, p2 + d, 0, 6, r2.at[4 * k + i])
            forward(i, q1, p2 + d, lambda j: s2.at[4 * k + j], lambda j: r2.at[4 * k + j], 2)
            share(4 * k + 1 + i, q1, p2 + d)

    def end_second(k):
        q1 = p1 + offs[k]
        expect(q1, p2 + 2, 0, 3, r2.at[4 * k + 2])
        expect(q1, p2 + 2, 3, 6, r2.at[4 * k + 3])
        share(4 * k + 3, q1, p2 + 2)

    def early(k):
        return (c == 0) & ((x + offs[k] + 4) % 4 < 2)

    def stage(first, step):
        for k in range(4):
            pick = early(k) if first else jnp.logical_not(early(k))

            @pl.when(pick)
            def _():
                step(k)

    ring_send(p1, p2, lambda i: s1.at[i], lambda i: r1.at[i], 1)
    half = z // 2

    @pl.when(z % 2 == c)
    def _():
        which = x // 2
        for j, ref in enumerate((hid_ref, tar_ref)):

            def column(b, carry):
                cols = pl.ds(pl.multiple_of(b * HD, HD), HD)

                def block(zz):
                    at = pl.multiple_of((b * 4 + zz) * HD, HD)
                    return ref.at[which, :, pl.ds(at, HD)]

                into = HY.at[j, half, :, cols]
                for d in (1, 2, 3):
                    to = (z + d) % 4
                    send(block(to), into, hs.at[j, d - 1], hr.at[j, half], dev(x, y, to, c))
                pltpu.make_async_copy(block(z), into, hr.at[j, half]).start()
                return carry

            lax.fori_loop(0, 8, column, 0)

    for i, d in enumerate((-1, 1)):
        expect(p1 + d, p2, 0, 6, r1.at[i])
        forward(i, p1 + d, p2, lambda j: s1.at[j], lambda j: r1.at[j], 1)
    expect(p1 + 2, p2, 0, 3, r1.at[2])
    expect(p1 + 2, p2, 3, 6, r1.at[3])
    stage(True, start_second)
    stage(True, relay_second)
    stage(False, start_second)
    stage(True, end_second)

    def shared(k):
        for i in range(4 * k, 4 * k + 4):
            ref = piece(W, p1, p2, 0, 6)
            pltpu.make_async_copy(ref, ref, r3.at[i]).wait()

    def from_other(first):
        for k in range(4):
            ahead = (c == 1) & ((x + offs[k] + 4) % 4 < 2)

            @pl.when(ahead if first else jnp.logical_not(ahead))
            def _():
                shared(k)

    from_other(True)

    def expect_rows(j):
        for i in range(2):
            pltpu.make_async_copy(HY.at[j, i], HY.at[j, i], hr.at[j, i]).wait()

    expect_rows(0)

    row = lax.broadcasted_iota(jnp.int32, (T, T), 0)
    col = lax.broadcasted_iota(jnp.int32, (T, T), 1)
    eye = row == col
    mask = (row >= col) & ((row < TOK) == (col < TOK))
    scale = 1.0 / math.sqrt(HD)

    def to_row(column):
        return jnp.sum(jnp.where(eye, column, 0.0), axis=0, keepdims=True)

    def to_column(line):
        return jnp.sum(jnp.where(eye, line, 0.0), axis=1, keepdims=True)

    def reduce_start(par, rows):
        copies = []
        for d in (1, 2, 3):
            copies.append(
                send(
                    snd.at[par, 0:rows], rcv.at[par, d - 1, 0:rows],
                    ars.at[par, d - 1], arr.at[par, d - 1], dev(x, y, (z + d) % 4, c),
                )
            )
        return copies

    def reduce_end(par, rows, copies):
        for copy in copies:
            copy.wait()
        total = snd[par, 0:rows].astype(F32)
        for d in range(3):
            total = total + rcv[par, d, 0:rows].astype(F32)
        return total

    def put(par, value, tangent):
        snd[par, 0:T, 0:R] = value.astype(BF16)
        snd[par, 0:T, R : 2 * R] = tangent.astype(BF16)

    chunks = [slice(j, j + CH) for j in range(0, C, CH)]

    def when(condition):
        return (lambda run: run()) if condition else (lambda run: None)

    def products(left, right):
        full = jnp.zeros((2 * T, 2 * R), F32)
        for ch in chunks:
            full = full + dot_nt(left(ch), right(ch))
        return cross(full)

    def later(par, lo, hi):
        return [
            pltpu.make_async_remote_copy(
                src_ref=bgs.at[par, :, lo:hi], dst_ref=bgr.at[par, d - 1, :, lo:hi],
                send_sem=bs.at[par, d - 1], recv_sem=br.at[par, d - 1],
                device_id=dev(x, y, (z + d) % 4, c), device_id_type=MESH,
            )
            for d in (1, 2, 3)
        ]

    def put_later(par, i, pair):
        bgs[par, :, 2 * i * R : (2 * i + 1) * R] = pair[0].astype(BF16)
        bgs[par, :, (2 * i + 1) * R : (2 * i + 2) * R] = pair[1].astype(BF16)

    def sum_later(par, i):
        cols = slice(2 * i * R, (2 * i + 2) * R)
        total = bgs[par, :, cols].astype(F32)
        for d in range(3):
            total = total + bgr[par, d, :, cols].astype(F32)
        return total

    for i in range(2):
        H2[0, i * TOK : (i + 1) * TOK] = HY[0, i]
    H2[0, T : 2 * T] = jnp.zeros((T, C), BF16)

    def latent_start(s):
        put(0, *products(lambda ch: H2[s, :, ch], lambda ch: W[s, 0, :, ch]))
        ss = jnp.zeros((T, 1), F32)
        st = jnp.zeros((T, 1), F32)
        for ch in chunks:
            hf = H2[s, 0:T, ch].astype(F32)
            ss = ss + jnp.sum(hf * hf, axis=1, keepdims=True)
            st = st + jnp.sum(hf * H2[s, T : 2 * T, ch].astype(F32), axis=1, keepdims=True)
        line = jnp.concatenate([to_row(ss), to_row(st)], 1)
        high = line.astype(BF16).astype(F32)
        place = lax.broadcasted_iota(jnp.int32, (16, 2 * T), 0)
        pair = jnp.where(place == 0, high, jnp.where(place == 1, line - high, 0.0))
        snd[0, T : T + 16, :] = pair.astype(BF16)
        return reduce_start(0, T + 16)

    def latent_end(s, copies):
        total = reduce_end(0, T + 16, copies)
        AS[s] = total[:T]
        line = jnp.sum(total[T:], axis=0, keepdims=True)
        SS[0] = jnp.broadcast_to(to_column(line[:, :T]), (T, R))
        SS[1] = jnp.broadcast_to(to_column(line[:, T:]), (T, R))

    copies = latent_start(0)
    stage(False, relay_second)
    expect_rows(1)
    for i in range(2):
        H2[5, i * TOK : (i + 1) * TOK] = HY[1, i]
    H2[5, T : 2 * T] = jnp.zeros((T, C), BF16)
    latent_end(0, copies)

    HR = R // 2
    RQ = R // 8
    first = pl.multiple_of(c * HR, HR)

    def own(s, right):
        full = jnp.zeros((2 * HR, 2 * R), F32)
        for ch in chunks:
            left = jnp.concatenate(
                [W[s, 5, pl.ds(first, HR), ch], W[s, 5, pl.ds(R + first, HR), ch]], 0
            )
            full = full + dot_nt(left, right(ch))
        return cross(full)

    def gram_products():
        for i in range(7):
            j = i % 4
            if i < 4:
                pair = own(j, lambda ch: W[j, 5, :, ch])
            else:
                pair = own(j, lambda ch: W[j + 1, 0, :, ch])
            for k in range(2):
                GP[:, (2 * i + k) * R : (2 * i + k + 1) * R] = pair[k].astype(BF16)

    def quarter(ref, zz):
        return ref.at[pl.ds(pl.multiple_of((zz % 4) * RQ, RQ), RQ)]

    gram_in, gram_out = [], []
    for d in (1, 2, 3):
        to = dev(x, y, (z + d) % 4, c)
        gram_in.append(
            pltpu.make_async_remote_copy(
                src_ref=quarter(GP, z + d), dst_ref=GV.at[d - 1],
                send_sem=gs.at[d - 1], recv_sem=gv.at[d - 1],
                device_id=to, device_id_type=MESH,
            )
        )
        gram_out.append(
            pltpu.make_async_remote_copy(
                src_ref=quarter(GA.at[c], z), dst_ref=quarter(GA.at[c], z),
                send_sem=gt.at[d - 1], recv_sem=ga.at[d - 1],
                device_id=to, device_id_type=MESH,
            )
        )
    gram_share = pltpu.make_async_remote_copy(
        src_ref=GA.at[c], dst_ref=GA.at[c], send_sem=gx.at[0], recv_sem=gx.at[1],
        device_id=sibling, device_id_type=MESH,
    )

    def gram_sum():
        total = quarter(GP, z)[...].astype(F32)
        for copy in gram_in:
            copy.wait()
        for d in range(3):
            total = total + GV[d].astype(F32)
        quarter(GA.at[c], z)[...] = total.astype(BF16)
        for copy in gram_out:
            copy.start()

    def gram_pass():
        for copy in gram_out:
            copy.wait()
        gram_share.start()

    def gram(i):
        cols = [slice((2 * i + k) * R, (2 * i + k + 1) * R) for k in range(2)]
        return jnp.concatenate([GA[h, :, cols[k]] for k in range(2) for h in range(2)], 0)

    def forward_layer(s, carry):
        par = s % 2
        slot = s % 2 if s > 0 else 1
        last = int(s == 3)
        lhs, layer, factor = s + 2 * last, s + 1 - last, 5 * last
        if s > 0:
            put_later(
                par, 0, products(lambda ch: H2[lhs, :, ch], lambda ch: W[layer, factor, :, ch])
            )
        put_later(par, 1, products(lambda ch: H2[s, :, ch], lambda ch: W[s, 5, :, ch]))
        others = later(par, 0 if s > 0 else 2 * R, 4 * R)
        for copy in others:
            copy.start()
        ss, st = SS[0, :, 0:1], SS[1, :, 0:1]
        r = lax.rsqrt(ss / D + EPS)
        rt = -(r * r * r) * st / D
        a, at = AS[s, :, 0:R], AS[s, :, R : 2 * R]
        RR[s, 0] = jnp.broadcast_to(r, (T, R))
        RR[s, 1] = jnp.broadcast_to(rt, (T, R))
        lat = (r * a).astype(BF16)
        latt = (r * at + rt * a).astype(BF16)
        LS[s, 0:T] = latt
        LS[s, T : 2 * T] = lat
        low = lower(lat, latt)
        for f in range(3):
            for ch in chunks:
                QKV[s, f, :, ch] = dot_nn(low, W[s, 2 + f, :, ch]).astype(BF16)

        if s == 1:
            gram_sum()

        def head(b, carry):
            cols = pl.ds(pl.multiple_of(b * HD, HD), HD)
            w, wt, mix = head_forward(
                QKV[s, 0, :, cols], QKV[s, 1, :, cols], QKV[s, 2, :, cols], mask, scale
            )
            AW[s, b, 0:T] = w
            AW[s, b, T : 2 * T] = wt
            MIX[s, :, cols] = mix.astype(BF16)
            return carry

        lax.fori_loop(0, 8, head, 0, unroll=True)
        put(slot, *products(lambda ch: MIX[s, :, ch], lambda ch: W[s, 1, :, ch]))
        copies = reduce_start(slot, T)
        if s == 0:
            stage(False, end_second)
        if s == 1:
            gram_pass()
        for copy in others:
            copy.wait()
        if s > 0:
            ZE[:, 0 : 2 * R] = sum_later(par, 0)
        ZE[:, 2 * R : 4 * R] = sum_later(par, 1)
        total = reduce_end(slot, T, copies)
        m, mt = total[:, :R].astype(BF16), total[:, R:].astype(BF16)
        MS[s, 0:T] = mt
        MS[s, T : 2 * T] = m
        low = lower(m, mt)
        for ch in chunks:
            H2[s + 1, :, ch] = (
                H2[s, :, ch].astype(F32) + dot_nn(low, W[s, 5, :, ch])
            ).astype(BF16)
        if s == 0:
            FS[0] = ZE[:, 2 * R : 4 * R]
            from_other(False)
            copies = latent_start(1)
            gram_products()
            for copy in gram_in:
                copy.start()
            latent_end(1, copies)
            return
        if s == 1:
            gram_share.wait()
            m0t, m0 = MS[0, 0:T], MS[0, T : 2 * T]
            k = dot_nn(lower(m0, m0t), gram(0))
            FS[0, :, 0:R] = FS[0, :, 0:R] + k[:T]
            FS[0, :, R : 2 * R] = FS[0, :, R : 2 * R] + k[T:]
        if s < 3:
            add = dot_nn(low, gram(4 + s))
            AS[s + 1, :, 0:R] = ZE[:, 0:R] + add[:T]
            AS[s + 1, :, R : 2 * R] = ZE[:, R : 2 * R] + add[T:]
        k = dot_nn(low, gram(s))
        k, kt = k[:T], k[T:]
        e, et = ZE[:, 2 * R : 3 * R], ZE[:, 3 * R : 4 * R]
        FS[s, :, 0:R] = e + k
        FS[s, :, R : 2 * R] = et + kt
        m, mt = m.astype(F32), mt.astype(F32)
        ss = ss + jnp.sum(m * (2.0 * e + k), axis=1, keepdims=True)
        st = st + jnp.sum(mt * e + m * et + 0.5 * (mt * k + m * kt), axis=1, keepdims=True)
        SS[0] = jnp.broadcast_to(ss, (T, R))
        SS[1] = jnp.broadcast_to(st, (T, R))
        return carry

    for s in range(4):
        forward_layer(s, 0)

    DMB[0:T] = ((FS[3, :, R : 2 * R] - ZE[:, R : 2 * R]) / count).astype(BF16)
    DMB[T : 2 * T] = ((FS[3, :, 0:R] - ZE[:, 0:R]) / count).astype(BF16)
    for ch in chunks:
        G2[0:T, ch] = (H2[4, 0:T, ch].astype(F32) - H2[5, 0:T, ch].astype(F32)) / count
        G2[T : 2 * T, ch] = H2[4, T : 2 * T, ch].astype(F32) / count

    def give(s, f0, f1, i):
        @pl.when(c != s % 2)
        def _():
            send(
                GR.at[s, f0:f1], RB0.at[s // 2, f0:f1], sa.at[s // 2, i], ra.at[s // 2, i], sibling
            )

    def add_other(hi):
        for i, (f0, f1) in enumerate(((1, 6), (0, 1))):
            ref = RB0.at[hi, f0:f1]
            pltpu.make_async_copy(ref, ref, ra.at[hi, i]).wait()

        def add(f, carry):
            here = GR[2 * hi + c, f].astype(F32) + RB0[hi, f].astype(F32)
            GR[2 * hi + c, f] = here.astype(BF16)
            return carry

        lax.fori_loop(0, 6, add, 0)

    def backward_layer(step, carry):
        s = 3 - step
        par = step % 2
        slot = step % 2
        others = later(par, 0, 2 * R) if s > 0 else []

        @when(s > 0)
        def _():
            put_later(
                par, 0, products(lambda ch: G2[:, ch].astype(BF16), lambda ch: W[s - 1, 5, :, ch])
            )
            for copy in others:
                copy.start()

        low = lower(DMB[T : 2 * T], DMB[0:T])
        for ch in chunks:
            DMIX[:, ch] = dot_nn(low, W[s, 1, :, ch]).astype(BF16)

        def head(b, carry):
            cols = pl.ds(pl.multiple_of(b * HD, HD), HD)
            dq, dk, dv = head_backward(
                QKV[s, 0, :, cols], QKV[s, 1, :, cols], QKV[s, 2, :, cols],
                AW[s, b, 0:T], AW[s, b, T : 2 * T], DMIX[:, cols], scale,
            )
            DX[0, :, cols] = dq.astype(BF16)
            DX[1, :, cols] = dk.astype(BF16)
            DX[2, :, cols] = dv.astype(BF16)
            return carry

        lax.fori_loop(0, 8, head, 0, unroll=True)
        full = jnp.zeros((2 * T, 2 * R), F32)
        for f in range(3):
            for ch in chunks:
                full = full + dot_nt(DX[f, :, ch], W[s, 2 + f, :, ch])
        put(slot, *cross(full))
        copies = reduce_start(slot, T)
        for ch in chunks:
            GR[s, 5, :, ch] = dot_tn(MS[s], G2[:, ch].astype(BF16)).astype(BF16)
            GR[s, 1, :, ch] = dot_tn(DMB[...], MIX[s, :, ch]).astype(BF16)
        for f in range(3):
            for ch in chunks:
                GR[s, 2 + f, :, ch] = dot_tn(LS[s], DX[f, :, ch]).astype(BF16)
        give(s, 1, 6, 0)
        if s == 0:
            add_other(1)

        @when(s > 0)
        def _():
            for copy in others:
                copy.wait()
            ZE[:, 0 : 2 * R] = sum_later(par, 0)

        total = reduce_end(slot, T, copies)
        dl, dlt = total[:, :R], total[:, R:]
        a, at = AS[s, :, 0:R], AS[s, :, R : 2 * R]
        r, rt = RR[s, 0, :, 0:1], RR[s, 1, :, 0:1]
        dot = jnp.sum(dl * a, axis=1, keepdims=True)
        dott = jnp.sum(dlt * a + dl * at, axis=1, keepdims=True)
        kap = r * r * r * dot / D
        kapt = (3.0 * r * r * rt * dot + r * r * r * dott) / D
        rl, rlt = (r * dl).astype(BF16), (rt * dl + r * dlt).astype(BF16)
        swapped = jnp.concatenate([dlt, dl], 0).astype(BF16)

        @when(s > 0)
        def _():
            v, t = cross(dot_nt(jnp.concatenate([rl, rlt], 0), gram(3 + s)))
            f, ft = FS[s - 1, :, 0:R], FS[s - 1, :, R : 2 * R]
            DMB[0:T] = (ZE[:, R : 2 * R] + t - kapt * f - kap * ft).astype(BF16)
            DMB[T : 2 * T] = (ZE[:, 0:R] + v - kap * f).astype(BF16)
            low = lower(rl, rlt)
            for ch in chunks:
                h = H2[s, 0:T, ch].astype(F32)
                ht = H2[s, T : 2 * T, ch].astype(F32)
                inner = dot_nn(low, W[s, 0, :, ch])
                G2[0:T, ch] = G2[0:T, ch] + inner[:T] - kap * h
                G2[T : 2 * T, ch] = G2[T : 2 * T, ch] + inner[T:] - kapt * h - kap * ht

        for ch in chunks:
            h = H2[s, 0:T, ch].astype(F32)
            ht = H2[s, T : 2 * T, ch].astype(F32)
            normed = jnp.concatenate([r * h, r * ht + rt * h], 0).astype(BF16)
            GR[s, 0, :, ch] = dot_tn(swapped, normed).astype(BF16)
        give(s, 0, 1, 1)
        return carry

    for step in range(4):
        backward_layer(step, 0)

    add_other(0)

    right, left = devp(p1 + 1, p2), devp(p1 - 1, p2)
    right2, left2 = devp(p1, p2 + 1), devp(p1, p2 - 1)
    order = (2, 1, -1, 0)
    ends = []
    halves = []
    for k, o in enumerate(order):
        q2 = p2 + o
        halves.append((
            send(piece(GR, p1 + 2, q2, 0, 3), RH.at[0, k], sb.at[0, k], rb.at[0, k], right),
            send(piece(GR, p1 + 2, q2, 3, 6), RH.at[1, k], sb.at[1, k], rb.at[1, k], left),
        ))
    wholes = []
    for k, o in enumerate(order):
        q2 = p2 + o
        pair = []
        for i, d in enumerate((1, -1)):
            halves[k][i].wait_recv()
            f0, f1 = ((0, 3), (3, 6))[i]
            there = piece(GR, p1 + d, q2, f0, f1)
            there[...] = (there[...].astype(F32) + RH[i, k].astype(F32)).astype(BF16)
            pair.append(
                send(
                    piece(GR, p1 + d, q2, 0, 6), RF.at[i, k], sb.at[2 + i, k], rb.at[2 + i, k],
                    (right, left)[i],
                )
            )
        wholes.append(pair)
    second = []
    for k, o in enumerate(order):
        for i in range(2):
            wholes[k][i].wait_recv()
        here = piece(GR, p1, p2 + o, 0, 6)
        total = here[...].astype(F32) + RF[0, k].astype(F32) + RF[1, k].astype(F32)
        P1[k] = total.astype(BF16)
        if k == 0:
            second.append(send(P1.at[0, 0:3], RH2.at[0], sc.at[0], rc.at[0], right2))
            second.append(send(P1.at[0, 3:6], RH2.at[1], sc.at[1], rc.at[1], left2))
        elif k <= 2:
            i = k - 1
            f0, f1 = ((0, 3), (3, 6))[i]
            second[i].wait_recv()
            P1[k, f0:f1] = (P1[k, f0:f1].astype(F32) + RH2[i].astype(F32)).astype(BF16)
            second.append(send(P1.at[k], RF2.at[i], sc.at[2 + i], rc.at[2 + i], (right2, left2)[i]))
    second[2].wait_recv()
    second[3].wait_recv()
    total = P1[3].astype(F32) + RF2[0].astype(F32) + RF2[1].astype(F32)
    out_ref[...] = total.astype(BF16)
    @pl.when(z % 2 == c)
    def _():
        for j in range(2):
            for d in range(3):
                ref = HY.at[j, half]
                pltpu.make_async_copy(ref, ref, hs.at[j, d]).wait()

    for hi in range(2):
        for i, (f0, f1) in enumerate(((1, 6), (0, 1))):
            ref = RB0.at[hi, f0:f1]
            pltpu.make_async_copy(ref, ref, sa.at[hi, i]).wait()

    for i in range(4):
        f1 = 6 if i < 2 else 3
        ref = piece(W, p1, p2, 0, f1)
        pltpu.make_async_copy(ref, ref, s1.at[i]).wait()
        for k in range(4):
            pltpu.make_async_copy(ref, ref, s2.at[4 * k + i]).wait()
    for i in range(16):
        ref = piece(W, p1, p2, 0, 6)
        pltpu.make_async_copy(ref, ref, s3.at[i]).wait()

    for group in (second, *halves, *wholes):
        for copy in group:
            copy.wait_send()


def body(hidden_in, targets, down_factors, up_factors, down_dir, up_dir):
    _, TOK, D = hidden_in.shape
    R, HD = down_factors.shape[2], down_factors.shape[3]
    T, C = 2 * TOK, 8 * HD
    count = 64.0 * TOK
    dma = pltpu.SemaphoreType.DMA
    vm = pltpu.VMEM
    out = pl.pallas_call(
        functools.partial(kernel, (R, HD, TOK, float(D), count)),
        out_shape=jax.ShapeDtypeStruct((6, R, HD), BF16),
        in_specs=[pl.BlockSpec(memory_space=pl.ANY)] * 6,
        out_specs=pl.BlockSpec(memory_space=vm),
        scratch_shapes=[
            vm((4, 6, 2 * R, C), BF16),
            vm((2, 2, TOK, C), BF16),
            vm((6, 2 * T, C), BF16),
            vm((4, 3, 2 * T, C), BF16),
            vm((4, 8, 2 * T, T), BF16),
            vm((4, 2 * T, C), BF16),
            vm((4, T, 2 * R), F32),
            vm((4, 2, T, R), F32),
            vm((4, 2 * T, R), BF16),
            vm((4, 2 * T, R), BF16),
            vm((2 * T, C), F32),
            vm((3, 2 * T, C), BF16),
            vm((2 * T, C), BF16),
            vm((4, 6, R, C), BF16),
            vm((2, T, R), F32),
            vm((4, T, 2 * R), F32),
            vm((R // 2, 14 * R), BF16),
            vm((3, R // 8, 14 * R), BF16),
            vm((2, R // 2, 14 * R), BF16),
            vm((T, 4 * R), F32),
            vm((2 * T, R), BF16),
            vm((2, T, 4 * R), BF16),
            vm((2, 3, T, 4 * R), BF16),
            dma((2, 3)), dma((2, 3)),
            dma((3,)), dma((3,)), dma((3,)), dma((3,)), dma((2,)),
            vm((2, T + 16, 2 * R), BF16),
            vm((2, 3, T + 16, 2 * R), BF16),
            vm((2, 6, R, C), BF16),
            vm((2, 4, 3, R, HD), BF16),
            vm((2, 4, 6, R, HD), BF16),
            vm((4, 6, R, HD), BF16),
            vm((2, 3, R, HD), BF16),
            vm((2, 6, R, HD), BF16),
            dma((4,)),
            dma((4,)), dma((4,)),
            dma((16,)), dma((16,)),
            dma((16,)), dma((16,)),
            dma((2, 3)), dma((2, 2)),
            dma((2, 3)), dma((2, 3)),
            dma((2, 2)), dma((2, 2)),
            dma((4, 4)), dma((4, 4)),
            dma((4,)), dma((4,)),
        ],
        compiler_params=pltpu.CompilerParams(
            collective_id=0, has_side_effects=True, vmem_limit_bytes=58 * 2**20
        ),
    )(hidden_in, targets, down_factors, up_factors, down_dir, up_dir)
    wide = out.astype(F32)
    return wide[None, 0:2], wide[None, 2:6]


def solution(mesh):
    in_specs = (
        P("dp", None, None),
        P("dp", None, None),
        P("section", None, None, "dp"),
        P("section", None, None, "dp"),
        P("section", None, None, "dp"),
        P("section", None, None, "dp"),
    )
    out_specs = (P("section", None, None, "dp"), P("section", None, None, "dp"))
    return jax.shard_map(body, mesh=mesh, in_specs=in_specs, out_specs=out_specs, check_vma=False)
```

```python
import functools
import math

import jax
import jax.numpy as jnp
from jax import lax
from jax.experimental import pallas as pl
from jax.experimental.pallas import tpu as pltpu
from jax.sharding import PartitionSpec as P

EPS = 1e-05
MESH = pl.DeviceIdType.MESH
F32 = jnp.float32
BF16 = jnp.bfloat16


def dot_nt(a, b):
    return lax.dot_general(a, b, (((1,), (1,)), ((), ())), preferred_element_type=F32)


def dot_tn(a, b):
    return lax.dot_general(a, b, (((0,), (0,)), ((), ())), preferred_element_type=F32)


def dot_nn(a, b):
    return lax.dot_general(a, b, (((1,), (0,)), ((), ())), preferred_element_type=F32)


def lower(a, at):
    return jnp.concatenate(
        [jnp.concatenate([a, jnp.zeros_like(a)], 1), jnp.concatenate([at, a], 1)], 0
    )


def cross(full):
    n, m = full.shape[0] // 2, full.shape[1] // 2
    return full[:n, :m], full[:n, m:] + full[n:, :m]


def head_forward(q2, k2, v2, mask, scale):
    s, st = cross(dot_nt(q2, k2))
    s = jnp.where(mask, s * scale, -1e30)
    st = st * scale
    e = jnp.exp(s - jnp.max(s, axis=-1, keepdims=True))
    w = e * (1.0 / jnp.sum(e, axis=-1, keepdims=True))
    wt = w * (st - jnp.sum(w * st, axis=-1, keepdims=True))
    w, wt = w.astype(BF16), wt.astype(BF16)
    return w, wt, dot_nn(lower(w, wt), v2)


def head_backward(q2, k2, v2, w, wt, dm2, scale):
    n = w.shape[0]
    da, dat = cross(dot_nt(dm2, v2))
    dvs = dot_tn(lower(w, wt), jnp.concatenate([dm2[n:], dm2[:n]], 0))
    wf, wtf = w.astype(F32), wt.astype(F32)
    da = da - jnp.sum(wf * da, axis=-1, keepdims=True)
    wda = wf * da
    dst = wtf * da + wf * dat
    dst = dst - wf * jnp.sum(dst, axis=-1, keepdims=True)
    ds = (wda * scale).astype(BF16)
    dst = (dst * scale).astype(BF16)
    low = lower(ds, dst)
    dq2 = dot_nn(low, k2)
    dks = dot_tn(low, jnp.concatenate([q2[n:], q2[:n]], 0))
    return (
        dq2,
        jnp.concatenate([dks[n:], dks[:n]], 0),
        jnp.concatenate([dvs[n:], dvs[:n]], 0),
    )


def kernel(
    dims,
    hid_ref, tar_ref, df_ref, uf_ref, dd_ref, ud_ref,
    out_ref,
    W, HY, H2, QKV, AW, MIX, AS, RR, MS, LS, G2, DX, DMIX, GR,
    SS, FS, GP, GV, GA, ZE, DMB, bgs, bgr, bs, br, gs, gv, gt, ga, gx,
    snd, rcv, RB0, RH, RF, P1, RH2, RF2,
    own_sem, s1, r1, s2, r2, s3, r3, hs, hr, ars, arr, sa, ra, sb, rb, sc, rc,
):
    R, HD, TOK, D, count = dims
    T = 2 * TOK
    C = 8 * HD
    CH = 2 * HD
    dp = lax.axis_index("dp")
    sec = lax.axis_index("section")
    x = 2 * (sec // 2) + dp // 16
    y = (dp // 4) % 4
    z = dp % 4
    c = sec % 2

    def dev(x, y, z, c):
        return ((x % 2) * 16 + y * 4 + z, (x // 2) * 2 + c)

    def to_xy(p1, p2):
        return p1 * (1 - c) + p2 * c, p2 * (1 - c) + p1 * c

    p1 = x * (1 - c) + y * c
    p2 = y * (1 - c) + x * c

    def devp(q1, q2):
        xx, yy = to_xy(q1 % 4, q2 % 4)
        return dev(xx, yy, z, c)

    def piece(ref, q1, q2, f0, f1):
        xx, yy = to_xy(q1 % 4, q2 % 4)
        col = pl.multiple_of(((xx % 2) * 4 + yy) * HD, HD)
        return ref.at[2 * (xx // 2) + c, f0:f1, :, pl.ds(col, HD)]

    sibling = dev(x, y, z, 1 - c)

    def send(src, dst, ssem, rsem, to):
        copy = pltpu.make_async_remote_copy(
            src_ref=src, dst_ref=dst, send_sem=ssem, recv_sem=rsem,
            device_id=to, device_id_type=MESH,
        )
        copy.start()
        return copy

    mine = [
        pltpu.make_async_copy(df_ref.at[0], piece(W, p1, p2, 0, 2).at[:, 0:R], own_sem.at[0]),
        pltpu.make_async_copy(dd_ref.at[0], piece(W, p1, p2, 0, 2).at[:, R : 2 * R], own_sem.at[1]),
        pltpu.make_async_copy(uf_ref.at[0], piece(W, p1, p2, 2, 6).at[:, 0:R], own_sem.at[2]),
        pltpu.make_async_copy(ud_ref.at[0], piece(W, p1, p2, 2, 6).at[:, R : 2 * R], own_sem.at[3]),
    ]
    for copy in mine:
        copy.start()

    barrier = pltpu.get_barrier_semaphore()
    peers = [
        devp(p1 + 1, p2), devp(p1 - 1, p2), devp(p1, p2 + 1), devp(p1, p2 - 1), sibling,
        dev(x, y, (z + 1) % 4, c), dev(x, y, (z + 2) % 4, c), dev(x, y, (z + 3) % 4, c),
    ]
    for peer in peers:
        pl.semaphore_signal(barrier, inc=1, device_id=peer, device_id_type=MESH)
    pl.semaphore_wait(barrier, len(peers))

    for copy in mine:
        copy.wait()


    def ring_send(q1, q2, ssem, rsem, axis):
        for i, d in enumerate((1, -1)):
            to = devp(p1 + d, p2) if axis == 1 else devp(p1, p2 + d)
            send(piece(W, q1, q2, 0, 6), piece(W, q1, q2, 0, 6), ssem(i), rsem(i), to)

    def forward(i, q1, q2, ssem, rsem, axis):
        d = (1, -1)[i]
        to = devp(p1 + d, p2) if axis == 1 else devp(p1, p2 + d)
        f0, f1 = ((0, 3), (3, 6))[i]
        send(piece(W, q1, q2, f0, f1), piece(W, q1, q2, f0, f1), ssem(2 + i), rsem(2 + i), to)

    def expect(q1, q2, f0, f1, rsem):
        ref = piece(W, q1, q2, f0, f1)
        pltpu.make_async_copy(ref, ref, rsem).wait()

    def share(i, q1, q2):
        send(piece(W, q1, q2, 0, 6), piece(W, q1, q2, 0, 6), s3.at[i], r3.at[i], sibling)

    offs = (0, -1, 1, 2)

    def start_second(k):
        q1 = p1 + offs[k]
        ring_send(q1, p2, lambda i: s2.at[4 * k + i], lambda i: r2.at[4 * k + i], 2)
        share(4 * k, q1, p2)

    def relay_second(k):
        q1 = p1 + offs[k]
        for i, d in enumerate((-1, 1)):
            expect(q1, p2 + d, 0, 6, r2.at[4 * k + i])
            forward(i, q1, p2 + d, lambda j: s2.at[4 * k + j], lambda j: r2.at[4 * k + j], 2)
            share(4 * k + 1 + i, q1, p2 + d)

    def end_second(k):
        q1 = p1 + offs[k]
        expect(q1, p2 + 2, 0, 3, r2.at[4 * k + 2])
        expect(q1, p2 + 2, 3, 6, r2.at[4 * k + 3])
        share(4 * k + 3, q1, p2 + 2)

    def early(k):
        return (c == 0) & ((x + offs[k] + 4) % 4 < 2)

    def stage(first, step):
        for k in range(4):
            pick = early(k) if first else jnp.logical_not(early(k))

            @pl.when(pick)
            def _():
                step(k)

    ring_send(p1, p2, lambda i: s1.at[i], lambda i: r1.at[i], 1)
    half = z // 2

    @pl.when(z % 2 == c)
    def _():
        which = x // 2
        for j, ref in enumerate((hid_ref, tar_ref)):

            def column(b, carry):
                cols = pl.ds(pl.multiple_of(b * HD, HD), HD)

                def block(zz):
                    at = pl.multiple_of((b * 4 + zz) * HD, HD)
                    return ref.at[which, :, pl.ds(at, HD)]

                into = HY.at[j, half, :, cols]
                for d in (1, 2, 3):
                    to = (z + d) % 4
                    send(block(to), into, hs.at[j, d - 1], hr.at[j, half], dev(x, y, to, c))
                pltpu.make_async_copy(block(z), into, hr.at[j, half]).start()
                return carry

            lax.fori_loop(0, 8, column, 0)

    for i, d in enumerate((-1, 1)):
        expect(p1 + d, p2, 0, 6, r1.at[i])
        forward(i, p1 + d, p2, lambda j: s1.at[j], lambda j: r1.at[j], 1)
    expect(p1 + 2, p2, 0, 3, r1.at[2])
    expect(p1 + 2, p2, 3, 6, r1.at[3])
    stage(True, start_second)
    stage(True, relay_second)
    stage(False, start_second)
    stage(True, end_second)

    def shared(k):
        for i in range(4 * k, 4 * k + 4):
            ref = piece(W, p1, p2, 0, 6)
            pltpu.make_async_copy(ref, ref, r3.at[i]).wait()

    def from_other(first):
        for k in range(4):
            ahead = (c == 1) & ((x + offs[k] + 4) % 4 < 2)

            @pl.when(ahead if first else jnp.logical_not(ahead))
            def _():
                shared(k)

    from_other(True)

    def expect_rows(j):
        for i in range(2):
            pltpu.make_async_copy(HY.at[j, i], HY.at[j, i], hr.at[j, i]).wait()

    expect_rows(0)

    row = lax.broadcasted_iota(jnp.int32, (T, T), 0)
    col = lax.broadcasted_iota(jnp.int32, (T, T), 1)
    eye = row == col
    mask = (row >= col) & ((row < TOK) == (col < TOK))
    scale = 1.0 / math.sqrt(HD)

    def to_row(column):
        return jnp.sum(jnp.where(eye, column, 0.0), axis=0, keepdims=True)

    def to_column(line):
        return jnp.sum(jnp.where(eye, line, 0.0), axis=1, keepdims=True)

    def reduce_start(par, rows):
        copies = []
        for d in (1, 2, 3):
            copies.append(
                send(
                    snd.at[par, 0:rows], rcv.at[par, d - 1, 0:rows],
                    ars.at[par, d - 1], arr.at[par, d - 1], dev(x, y, (z + d) % 4, c),
                )
            )
        return copies

    def reduce_end(par, rows, copies):
        for copy in copies:
            copy.wait()
        total = snd[par, 0:rows].astype(F32)
        for d in range(3):
            total = total + rcv[par, d, 0:rows].astype(F32)
        return total

    def put(par, value, tangent):
        snd[par, 0:T, 0:R] = value.astype(BF16)
        snd[par, 0:T, R : 2 * R] = tangent.astype(BF16)

    chunks = [slice(j, j + CH) for j in range(0, C, CH)]

    def when(condition):
        return (lambda run: run()) if condition else (lambda run: None)

    def products(left, right):
        full = jnp.zeros((2 * T, 2 * R), F32)
        for ch in chunks:
            full = full + dot_nt(left(ch), right(ch))
        return cross(full)

    def later(par, lo, hi):
        return [
            pltpu.make_async_remote_copy(
                src_ref=bgs.at[par, :, lo:hi], dst_ref=bgr.at[par, d - 1, :, lo:hi],
                send_sem=bs.at[par, d - 1], recv_sem=br.at[par, d - 1],
                device_id=dev(x, y, (z + d) % 4, c), device_id_type=MESH,
            )
            for d in (1, 2, 3)
        ]

    def put_later(par, i, pair):
        bgs[par, :, 2 * i * R : (2 * i + 1) * R] = pair[0].astype(BF16)
        bgs[par, :, (2 * i + 1) * R : (2 * i + 2) * R] = pair[1].astype(BF16)

    def sum_later(par, i):
        cols = slice(2 * i * R, (2 * i + 2) * R)
        total = bgs[par, :, cols].astype(F32)
        for d in range(3):
            total = total + bgr[par, d, :, cols].astype(F32)
        return total

    for i in range(2):
        H2[0, i * TOK : (i + 1) * TOK] = HY[0, i]
    H2[0, T : 2 * T] = jnp.zeros((T, C), BF16)

    def latent_start(s):
        put(0, *products(lambda ch: H2[s, :, ch], lambda ch: W[s, 0, :, ch]))
        ss = jnp.zeros((T, 1), F32)
        st = jnp.zeros((T, 1), F32)
        for ch in chunks:
            hf = H2[s, 0:T, ch].astype(F32)
            ss = ss + jnp.sum(hf * hf, axis=1, keepdims=True)
            st = st + jnp.sum(hf * H2[s, T : 2 * T, ch].astype(F32), axis=1, keepdims=True)
        line = jnp.concatenate([to_row(ss), to_row(st)], 1)
        high = line.astype(BF16).astype(F32)
        place = lax.broadcasted_iota(jnp.int32, (16, 2 * T), 0)
        pair = jnp.where(place == 0, high, jnp.where(place == 1, line - high, 0.0))
        snd[0, T : T + 16, :] = pair.astype(BF16)
        return reduce_start(0, T + 16)

    def latent_end(s, copies):
        total = reduce_end(0, T + 16, copies)
        AS[s] = total[:T]
        line = jnp.sum(total[T:], axis=0, keepdims=True)
        SS[0] = jnp.broadcast_to(to_column(line[:, :T]), (T, R))
        SS[1] = jnp.broadcast_to(to_column(line[:, T:]), (T, R))

    copies = latent_start(0)
    stage(False, relay_second)
    expect_rows(1)
    for i in range(2):
        H2[5, i * TOK : (i + 1) * TOK] = HY[1, i]
    H2[5, T : 2 * T] = jnp.zeros((T, C), BF16)
    latent_end(0, copies)

    HR = R // 2
    RQ = R // 8
    first = pl.multiple_of(c * HR, HR)

    def own(s, right):
        full = jnp.zeros((2 * HR, 2 * R), F32)
        for ch in chunks:
            left = jnp.concatenate(
                [W[s, 5, pl.ds(first, HR), ch], W[s, 5, pl.ds(R + first, HR), ch]], 0
            )
            full = full + dot_nt(left, right(ch))
        return cross(full)

    def gram_products():
        for i in range(7):
            j = i % 4
            if i < 4:
                pair = own(j, lambda ch: W[j, 5, :, ch])
            else:
                pair = own(j, lambda ch: W[j + 1, 0, :, ch])
            for k in range(2):
                GP[:, (2 * i + k) * R : (2 * i + k + 1) * R] = pair[k].astype(BF16)

    def quarter(ref, zz):
        return ref.at[pl.ds(pl.multiple_of((zz % 4) * RQ, RQ), RQ)]

    gram_in, gram_out = [], []
    for d in (1, 2, 3):
        to = dev(x, y, (z + d) % 4, c)
        gram_in.append(
            pltpu.make_async_remote_copy(
                src_ref=quarter(GP, z + d), dst_ref=GV.at[d - 1],
                send_sem=gs.at[d - 1], recv_sem=gv.at[d - 1],
                device_id=to, device_id_type=MESH,
            )
        )
        gram_out.append(
            pltpu.make_async_remote_copy(
                src_ref=quarter(GA.at[c], z), dst_ref=quarter(GA.at[c], z),
                send_sem=gt.at[d - 1], recv_sem=ga.at[d - 1],
                device_id=to, device_id_type=MESH,
            )
        )
    gram_share = pltpu.make_async_remote_copy(
        src_ref=GA.at[c], dst_ref=GA.at[c], send_sem=gx.at[0], recv_sem=gx.at[1],
        device_id=sibling, device_id_type=MESH,
    )

    def gram_sum():
        total = quarter(GP, z)[...].astype(F32)
        for copy in gram_in:
            copy.wait()
        for d in range(3):
            total = total + GV[d].astype(F32)
        quarter(GA.at[c], z)[...] = total.astype(BF16)
        for copy in gram_out:
            copy.start()

    def gram_pass():
        for copy in gram_out:
            copy.wait()
        gram_share.start()

    def gram(i):
        cols = [slice((2 * i + k) * R, (2 * i + k + 1) * R) for k in range(2)]
        return jnp.concatenate([GA[h, :, cols[k]] for k in range(2) for h in range(2)], 0)

    def forward_layer(s, carry):
        par = s % 2
        slot = s % 2 if s > 0 else 1
        last = int(s == 3)
        lhs, layer, factor = s + 2 * last, s + 1 - last, 5 * last
        if s > 0:
            put_later(
                par, 0, products(lambda ch: H2[lhs, :, ch], lambda ch: W[layer, factor, :, ch])
            )
        put_later(par, 1, products(lambda ch: H2[s, :, ch], lambda ch: W[s, 5, :, ch]))
        others = later(par, 0 if s > 0 else 2 * R, 4 * R)
        for copy in others:
            copy.start()
        ss, st = SS[0, :, 0:1], SS[1, :, 0:1]
        r = lax.rsqrt(ss / D + EPS)
        rt = -(r * r * r) * st / D
        a, at = AS[s, :, 0:R], AS[s, :, R : 2 * R]
        RR[s, 0] = jnp.broadcast_to(r, (T, R))
        RR[s, 1] = jnp.broadcast_to(rt, (T, R))
        lat = (r * a).astype(BF16)
        latt = (r * at + rt * a).astype(BF16)
        LS[s, 0:T] = latt
        LS[s, T : 2 * T] = lat
        low = lower(lat, latt)
        for f in range(3):
            for ch in chunks:
                QKV[s, f, :, ch] = dot_nn(low, W[s, 2 + f, :, ch]).astype(BF16)

        if s == 1:
            gram_sum()

        def head(b, carry):
            cols = pl.ds(pl.multiple_of(b * HD, HD), HD)
            w, wt, mix = head_forward(
                QKV[s, 0, :, cols], QKV[s, 1, :, cols], QKV[s, 2, :, cols], mask, scale
            )
            AW[s, b, 0:T] = w
            AW[s, b, T : 2 * T] = wt
            MIX[s, :, cols] = mix.astype(BF16)
            return carry

        lax.fori_loop(0, 8, head, 0, unroll=True)
        put(slot, *products(lambda ch: MIX[s, :, ch], lambda ch: W[s, 1, :, ch]))
        copies = reduce_start(slot, T)
        if s == 0:
            stage(False, end_second)
        if s == 1:
            gram_pass()
        for copy in others:
            copy.wait()
        if s > 0:
            ZE[:, 0 : 2 * R] = sum_later(par, 0)
        ZE[:, 2 * R : 4 * R] = sum_later(par, 1)
        total = reduce_end(slot, T, copies)
        m, mt = total[:, :R].astype(BF16), total[:, R:].astype(BF16)
        MS[s, 0:T] = mt
        MS[s, T : 2 * T] = m
        low = lower(m, mt)
        for ch in chunks:
            H2[s + 1, :, ch] = (
                H2[s, :, ch].astype(F32) + dot_nn(low, W[s, 5, :, ch])
            ).astype(BF16)
        if s == 0:
            FS[0] = ZE[:, 2 * R : 4 * R]
            from_other(False)
            copies = latent_start(1)
            gram_products()
            for copy in gram_in:
                copy.start()
            latent_end(1, copies)
            return
        if s == 1:
            gram_share.wait()
            m0t, m0 = MS[0, 0:T], MS[0, T : 2 * T]
            k = dot_nn(lower(m0, m0t), gram(0))
            FS[0, :, 0:R] = FS[0, :, 0:R] + k[:T]
            FS[0, :, R : 2 * R] = FS[0, :, R : 2 * R] + k[T:]
        if s < 3:
            add = dot_nn(low, gram(4 + s))
            AS[s + 1, :, 0:R] = ZE[:, 0:R] + add[:T]
            AS[s + 1, :, R : 2 * R] = ZE[:, R : 2 * R] + add[T:]
        k = dot_nn(low, gram(s))
        k, kt = k[:T], k[T:]
        e, et = ZE[:, 2 * R : 3 * R], ZE[:, 3 * R : 4 * R]
        FS[s, :, 0:R] = e + k
        FS[s, :, R : 2 * R] = et + kt
        m, mt = m.astype(F32), mt.astype(F32)
        ss = ss + jnp.sum(m * (2.0 * e + k), axis=1, keepdims=True)
        st = st + jnp.sum(mt * e + m * et + 0.5 * (mt * k + m * kt), axis=1, keepdims=True)
        SS[0] = jnp.broadcast_to(ss, (T, R))
        SS[1] = jnp.broadcast_to(st, (T, R))
        return carry

    for s in range(4):
        forward_layer(s, 0)

    DMB[0:T] = ((FS[3, :, R : 2 * R] - ZE[:, R : 2 * R]) * (1.0 / count)).astype(BF16)
    DMB[T : 2 * T] = ((FS[3, :, 0:R] - ZE[:, 0:R]) * (1.0 / count)).astype(BF16)
    for ch in chunks:
        G2[0:T, ch] = (H2[4, 0:T, ch].astype(F32) - H2[5, 0:T, ch].astype(F32)) * (1.0 / count)
        G2[T : 2 * T, ch] = H2[4, T : 2 * T, ch].astype(F32) * (1.0 / count)

    def give(s, f0, f1, i):
        @pl.when(c != s % 2)
        def _():
            send(
                GR.at[s, f0:f1], RB0.at[s // 2, f0:f1], sa.at[s // 2, i], ra.at[s // 2, i], sibling
            )

    def add_other(hi):
        for i, (f0, f1) in enumerate(((1, 6), (0, 1))):
            ref = RB0.at[hi, f0:f1]
            pltpu.make_async_copy(ref, ref, ra.at[hi, i]).wait()

        def add(f, carry):
            here = GR[2 * hi + c, f].astype(F32) + RB0[hi, f].astype(F32)
            GR[2 * hi + c, f] = here.astype(BF16)
            return carry

        lax.fori_loop(0, 6, add, 0)

    def backward_layer(step, carry):
        s = 3 - step
        par = step % 2
        slot = step % 2
        others = later(par, 0, 2 * R) if s > 0 else []

        @when(s > 0)
        def _():
            put_later(
                par, 0, products(lambda ch: G2[:, ch].astype(BF16), lambda ch: W[s - 1, 5, :, ch])
            )
            for copy in others:
                copy.start()

        low = lower(DMB[T : 2 * T], DMB[0:T])
        for ch in chunks:
            DMIX[:, ch] = dot_nn(low, W[s, 1, :, ch]).astype(BF16)

        def head(b, carry):
            cols = pl.ds(pl.multiple_of(b * HD, HD), HD)
            dq, dk, dv = head_backward(
                QKV[s, 0, :, cols], QKV[s, 1, :, cols], QKV[s, 2, :, cols],
                AW[s, b, 0:T], AW[s, b, T : 2 * T], DMIX[:, cols], scale,
            )
            DX[0, :, cols] = dq.astype(BF16)
            DX[1, :, cols] = dk.astype(BF16)
            DX[2, :, cols] = dv.astype(BF16)
            return carry

        lax.fori_loop(0, 8, head, 0, unroll=True)
        full = jnp.zeros((2 * T, 2 * R), F32)
        for f in range(3):
            for ch in chunks:
                full = full + dot_nt(DX[f, :, ch], W[s, 2 + f, :, ch])
        put(slot, *cross(full))
        copies = reduce_start(slot, T)
        for ch in chunks:
            GR[s, 5, :, ch] = dot_tn(MS[s], G2[:, ch].astype(BF16)).astype(BF16)
            GR[s, 1, :, ch] = dot_tn(DMB[...], MIX[s, :, ch]).astype(BF16)
        for f in range(3):
            for ch in chunks:
                GR[s, 2 + f, :, ch] = dot_tn(LS[s], DX[f, :, ch]).astype(BF16)
        give(s, 1, 6, 0)
        if s == 0:
            add_other(1)

        @when(s > 0)
        def _():
            for copy in others:
                copy.wait()
            ZE[:, 0 : 2 * R] = sum_later(par, 0)

        total = reduce_end(slot, T, copies)
        dl, dlt = total[:, :R], total[:, R:]
        a, at = AS[s, :, 0:R], AS[s, :, R : 2 * R]
        r, rt = RR[s, 0, :, 0:1], RR[s, 1, :, 0:1]
        dot = jnp.sum(dl * a, axis=1, keepdims=True)
        dott = jnp.sum(dlt * a + dl * at, axis=1, keepdims=True)
        kap = r * r * r * dot / D
        kapt = (3.0 * r * r * rt * dot + r * r * r * dott) / D
        rl, rlt = (r * dl).astype(BF16), (rt * dl + r * dlt).astype(BF16)
        swapped = jnp.concatenate([dlt, dl], 0).astype(BF16)

        @when(s > 0)
        def _():
            v, t = cross(dot_nt(jnp.concatenate([rl, rlt], 0), gram(3 + s)))
            f, ft = FS[s - 1, :, 0:R], FS[s - 1, :, R : 2 * R]
            DMB[0:T] = (ZE[:, R : 2 * R] + t - kapt * f - kap * ft).astype(BF16)
            DMB[T : 2 * T] = (ZE[:, 0:R] + v - kap * f).astype(BF16)
            low = lower(rl, rlt)
            for ch in chunks:
                h = H2[s, 0:T, ch].astype(F32)
                ht = H2[s, T : 2 * T, ch].astype(F32)
                inner = dot_nn(low, W[s, 0, :, ch])
                G2[0:T, ch] = G2[0:T, ch] + inner[:T] - kap * h
                G2[T : 2 * T, ch] = G2[T : 2 * T, ch] + inner[T:] - kapt * h - kap * ht

        for ch in chunks:
            h = H2[s, 0:T, ch].astype(F32)
            ht = H2[s, T : 2 * T, ch].astype(F32)
            normed = jnp.concatenate([r * h, r * ht + rt * h], 0).astype(BF16)
            GR[s, 0, :, ch] = dot_tn(swapped, normed).astype(BF16)
        give(s, 0, 1, 1)
        return carry

    for step in range(4):
        backward_layer(step, 0)

    add_other(0)

    right, left = devp(p1 + 1, p2), devp(p1 - 1, p2)
    right2, left2 = devp(p1, p2 + 1), devp(p1, p2 - 1)
    order = (2, 1, -1, 0)
    ends = []
    halves = []
    for k, o in enumerate(order):
        q2 = p2 + o
        halves.append((
            send(piece(GR, p1 + 2, q2, 0, 3), RH.at[0, k], sb.at[0, k], rb.at[0, k], right),
            send(piece(GR, p1 + 2, q2, 3, 6), RH.at[1, k], sb.at[1, k], rb.at[1, k], left),
        ))
    wholes = []
    for k, o in enumerate(order):
        q2 = p2 + o
        pair = []
        for i, d in enumerate((1, -1)):
            halves[k][i].wait_recv()
            f0, f1 = ((0, 3), (3, 6))[i]
            there = piece(GR, p1 + d, q2, f0, f1)
            there[...] = (there[...].astype(F32) + RH[i, k].astype(F32)).astype(BF16)
            pair.append(
                send(
                    piece(GR, p1 + d, q2, 0, 6), RF.at[i, k], sb.at[2 + i, k], rb.at[2 + i, k],
                    (right, left)[i],
                )
            )
        wholes.append(pair)
    second = []
    for k, o in enumerate(order):
        for i in range(2):
            wholes[k][i].wait_recv()
        here = piece(GR, p1, p2 + o, 0, 6)
        total = here[...].astype(F32) + RF[0, k].astype(F32) + RF[1, k].astype(F32)
        P1[k] = total.astype(BF16)
        if k == 0:
            second.append(send(P1.at[0, 0:3], RH2.at[0], sc.at[0], rc.at[0], right2))
            second.append(send(P1.at[0, 3:6], RH2.at[1], sc.at[1], rc.at[1], left2))
        elif k <= 2:
            i = k - 1
            f0, f1 = ((0, 3), (3, 6))[i]
            second[i].wait_recv()
            P1[k, f0:f1] = (P1[k, f0:f1].astype(F32) + RH2[i].astype(F32)).astype(BF16)
            second.append(send(P1.at[k], RF2.at[i], sc.at[2 + i], rc.at[2 + i], (right2, left2)[i]))
    second[2].wait_recv()
    second[3].wait_recv()
    total = P1[3].astype(F32) + RF2[0].astype(F32) + RF2[1].astype(F32)
    out_ref[...] = total.astype(BF16)
    @pl.when(z % 2 == c)
    def _():
        for j in range(2):
            for d in range(3):
                ref = HY.at[j, half]
                pltpu.make_async_copy(ref, ref, hs.at[j, d]).wait()

    for hi in range(2):
        for i, (f0, f1) in enumerate(((1, 6), (0, 1))):
            ref = RB0.at[hi, f0:f1]
            pltpu.make_async_copy(ref, ref, sa.at[hi, i]).wait()

    for i in range(4):
        f1 = 6 if i < 2 else 3
        ref = piece(W, p1, p2, 0, f1)
        pltpu.make_async_copy(ref, ref, s1.at[i]).wait()
        for k in range(4):
            pltpu.make_async_copy(ref, ref, s2.at[4 * k + i]).wait()
    for i in range(16):
        ref = piece(W, p1, p2, 0, 6)
        pltpu.make_async_copy(ref, ref, s3.at[i]).wait()

    for group in (second, *halves, *wholes):
        for copy in group:
            copy.wait_send()


def body(hidden_in, targets, down_factors, up_factors, down_dir, up_dir):
    _, TOK, D = hidden_in.shape
    R, HD = down_factors.shape[2], down_factors.shape[3]
    T, C = 2 * TOK, 8 * HD
    count = 64.0 * TOK
    dma = pltpu.SemaphoreType.DMA
    vm = pltpu.VMEM
    out = pl.pallas_call(
        functools.partial(kernel, (R, HD, TOK, float(D), count)),
        out_shape=jax.ShapeDtypeStruct((6, R, HD), BF16),
        in_specs=[pl.BlockSpec(memory_space=pl.ANY)] * 6,
        out_specs=pl.BlockSpec(memory_space=vm),
        scratch_shapes=[
            vm((4, 6, 2 * R, C), BF16),
            vm((2, 2, TOK, C), BF16),
            vm((6, 2 * T, C), BF16),
            vm((4, 3, 2 * T, C), BF16),
            vm((4, 8, 2 * T, T), BF16),
            vm((4, 2 * T, C), BF16),
            vm((4, T, 2 * R), F32),
            vm((4, 2, T, R), F32),
            vm((4, 2 * T, R), BF16),
            vm((4, 2 * T, R), BF16),
            vm((2 * T, C), F32),
            vm((3, 2 * T, C), BF16),
            vm((2 * T, C), BF16),
            vm((4, 6, R, C), BF16),
            vm((2, T, R), F32),
            vm((4, T, 2 * R), F32),
            vm((R // 2, 14 * R), BF16),
            vm((3, R // 8, 14 * R), BF16),
            vm((2, R // 2, 14 * R), BF16),
            vm((T, 4 * R), F32),
            vm((2 * T, R), BF16),
            vm((2, T, 4 * R), BF16),
            vm((2, 3, T, 4 * R), BF16),
            dma((2, 3)), dma((2, 3)),
            dma((3,)), dma((3,)), dma((3,)), dma((3,)), dma((2,)),
            vm((2, T + 16, 2 * R), BF16),
            vm((2, 3, T + 16, 2 * R), BF16),
            vm((2, 6, R, C), BF16),
            vm((2, 4, 3, R, HD), BF16),
            vm((2, 4, 6, R, HD), BF16),
            vm((4, 6, R, HD), BF16),
            vm((2, 3, R, HD), BF16),
            vm((2, 6, R, HD), BF16),
            dma((4,)),
            dma((4,)), dma((4,)),
            dma((16,)), dma((16,)),
            dma((16,)), dma((16,)),
            dma((2, 3)), dma((2, 2)),
            dma((2, 3)), dma((2, 3)),
            dma((2, 2)), dma((2, 2)),
            dma((4, 4)), dma((4, 4)),
            dma((4,)), dma((4,)),
        ],
        compiler_params=pltpu.CompilerParams(
            collective_id=0, has_side_effects=True, vmem_limit_bytes=58 * 2**20
        ),
    )(hidden_in, targets, down_factors, up_factors, down_dir, up_dir)
    wide = out.astype(F32)
    return wide[None, 0:2], wide[None, 2:6]


def solution(mesh):
    in_specs = (
        P("dp", None, None),
        P("dp", None, None),
        P("section", None, None, "dp"),
        P("section", None, None, "dp"),
        P("section", None, None, "dp"),
        P("section", None, None, "dp"),
    )
    out_specs = (P("section", None, None, "dp"), P("section", None, None, "dp"))
    return jax.shard_map(body, mesh=mesh, in_specs=in_specs, out_specs=out_specs, check_vma=False)
```
